256 devices in a mesh: rows: 32 (over y, z), cols: 8 (over x, core).
Axes of the slice: x: 4, y: 4, z: 8, core: 2. Of those that a mesh axis runs over, the one named last changes fastest.
Arguments:
- omega: bfloat16 [65536, 256], P(('rows', 'cols')), may hold values from -6 to 6
- tiles: bfloat16 [32, 8, 64, 128, 128], P('rows', 'cols')
- coords: int32 [32, 8, 64, 2], P('rows', 'cols'), may hold values from -1 to 511, as said below
Outputs:
- basis: float32 [65536, 256], P(('rows', 'cols'))
- first_basis: float32 [65536, 256], P(('rows', 'cols'))
- second_basis: float32 [65536, 256], P(('rows', 'cols'))
The draws below stay inside these ranges and needn't reach their ends.
Inputs may be any that keep to these rules, and one draw needn't show every extreme that they name: `coords`: slots of one device name blocks whose block row lies in that device's rows range of 16 block rows and whose block column c satisfies (c // 2) % 8 equal to its cols index; no position repeats on a device; live slots come first and padded slots hold -1 in both entries; some device has all 64 slots live, every device at least 16.
All inputs are finite; a program needn't handle non-finite values.
Results may differ from the reference program's by a relative error of at most 0.0026.
Values may be sent and summed in bfloat16 or wider, within the bound.
No kernel may reach another device: no remote copies, remote signals or barrier semaphores. Data moves between devices by JAX's collectives and lax.ppermute only.
A program may use at most 128 MiB of HBM per device.

```python
import math
import jax
import jax.numpy as jnp
from jax import lax

TILE = 128
K = 256
RB_DEV = 16
TILES_DEV = 64
NB = 512
CB = 64
PB = 2
N = 65536
N_ROWS = 32
N_COLS = 8


def draw_tiles(key, part):
    key = jax.random.fold_in(key, 11)
    first, second, third = jax.random.split(key, 3)
    shape = (N_ROWS, N_COLS, TILES_DEV, TILE, TILE)
    base = jax.random.normal(first, shape, jnp.float32)
    spread = 3.0
    row_scale = jnp.exp(jax.random.uniform(second, (N_ROWS, N_COLS, TILES_DEV, TILE, 1), jnp.float32) * jnp.log(spread))
    col_scale = jnp.exp(jax.random.uniform(third, (N_ROWS, N_COLS, TILES_DEV, 1, TILE), jnp.float32) * jnp.log(spread))
    return (base * row_scale * col_scale * 0.08).astype(jnp.bfloat16)


def draw_coords(key, part):
    key = jax.random.fold_in(key, 5)
    first, second, third = jax.random.split(key, 3)
    devices = N_ROWS * N_COLS
    slots = RB_DEV * CB
    keys = jax.random.split(first, devices)
    chosen = jax.vmap(lambda k: jax.random.permutation(k, slots)[:TILES_DEV])(keys).astype(jnp.int32)
    counts = jax.random.randint(second, (devices,), TILES_DEV // 4, TILES_DEV + 1).astype(jnp.int32)
    busy = jax.random.randint(third, (), 0, devices).astype(jnp.int32)
    device_ids = jnp.arange(devices, dtype=jnp.int32)
    counts = jnp.where(device_ids == busy, TILES_DEV, counts)
    live = jnp.arange(TILES_DEV, dtype=jnp.int32)[None, :] < counts[:, None]
    row_owner = device_ids // N_COLS
    col_owner = device_ids % N_COLS
    local_row = chosen // CB
    local_col = chosen % CB
    group = local_col // PB
    within = local_col % PB
    global_row = row_owner[:, None] * RB_DEV + local_row
    global_col = (group * N_COLS + col_owner[:, None]) * PB + within
    pairs = jnp.stack([jnp.where(live, global_row, -1), jnp.where(live, global_col, -1)], -1)
    return pairs.reshape(N_ROWS, N_COLS, TILES_DEV, 2).astype(jnp.int32)


def block_scale(stream_key, dims, cuts, smallest, high):
    loudness = 1.0
    for dim, shards_of in cuts:
        draws = jax.random.uniform(jax.random.fold_in(jax.random.fold_in(stream_key, 6), dim), (shards_of,), jnp.float32, smallest / len(cuts), high / len(cuts))
        loudness = loudness * jnp.repeat(jnp.exp(draws), dims[dim] // shards_of).reshape((-1,) + (1,) * (len(dims) - 1 - dim))
    return loudness


def bell_draw(own_key, dims, width, reach, pieces=(), held_as=jnp.bfloat16):
    gain = block_scale(own_key, dims, pieces, -0.22, 0.18) if pieces else 1.0
    drawn = jax.random.normal(own_key, dims, jnp.float32) * width * gain
    return jnp.minimum(jnp.maximum(drawn, -reach), reach).astype(held_as)


def setup_inputs(seed: int = 0) -> dict:
    arg_keys = jax.random.split(jax.random.key(seed), 4)
    omega = bell_draw(arg_keys[0], (N, K), 1.0, 6.0, ((0, 256),))
    tiles = draw_tiles(jax.random.fold_in(arg_keys[3], 71), 0)
    coords = draw_coords(jax.random.fold_in(arg_keys[3], 71), 0)
    return {"omega": omega, "tiles": tiles, "coords": coords}


highest = lax.Precision.HIGHEST

def multiply(panel, tiles, coords, transpose):
    blocks = panel.reshape(NB, TILE, K)
    flat_tiles = tiles.reshape(-1, TILES_DEV, TILE, TILE)
    flat_coords = coords.reshape(-1, TILES_DEV, 2)

    def step(total, item):
        tile_set, pairs = item
        live = (pairs[:, 0] >= 0).astype(jnp.float32)[:, None, None]
        block_rows = jnp.maximum(pairs[:, 0], 0).astype(jnp.int32)
        block_cols = jnp.maximum(pairs[:, 1], 0).astype(jnp.int32)
        if transpose:
            source = blocks[block_rows].astype(jnp.float32)
            prod = jnp.einsum('tji,tjk->tik', tile_set.astype(jnp.float32), source, precision=highest) * live
            return (total.at[block_cols].add(prod), None)
        source = blocks[block_cols].astype(jnp.float32)
        prod = jnp.einsum('tij,tjk->tik', tile_set.astype(jnp.float32), source, precision=highest) * live
        return (total.at[block_rows].add(prod), None)
    start = jnp.zeros((NB, TILE, K), jnp.float32)
    total, _ = lax.scan(step, start, (flat_tiles, flat_coords))
    return total.reshape(NB * TILE, K)

def orthonormal(panel):
    gram = lax.dot_general(panel, panel, (((0,), (0,)), ((), ())), precision=highest)
    lower = jnp.linalg.cholesky(gram)
    eye = jnp.eye(K, dtype=gram.dtype)
    inverse = lax.linalg.triangular_solve(lower, eye, left_side=True, lower=True)
    return lax.dot_general(panel, inverse, (((1,), (1,)), ((), ())), precision=highest)

def reference(omega, tiles, coords):
    factor = math.sqrt(NB * TILE)
    y_one = multiply(omega, tiles, coords, False)
    first = orthonormal(y_one)
    q_one = first.astype(jnp.bfloat16)
    z_two = multiply(q_one, tiles, coords, True)
    second = orthonormal(z_two)
    q_two = second.astype(jnp.bfloat16)
    y_three = multiply(q_two, tiles, coords, False)
    return (orthonormal(y_three) * factor, first * factor, second * factor)
```

```python
import functools
import math

import jax
import jax.numpy as jnp
from jax import lax
from jax.experimental import pallas as pl
from jax.experimental.pallas import tpu as pltpu
from jax.sharding import Mesh, PartitionSpec as P

highest = lax.Precision.HIGHEST
f32 = jnp.float32
bf16 = jnp.bfloat16
AXES = ("y", "z", "x", "core")
SIZE = {"y": 4, "z": 8, "x": 4, "core": 2}
GROUP = 4
BLOCK = 32
PIVOTS = 8
TAIL = 16
LEVELS = 16383.0
MIB = 1024 * 1024


def send(value, axis, step):
    size = SIZE[axis]
    return lax.ppermute(value, axis, [(i, (i + step) % size) for i in range(size)])


def ring_gather(piece, axis):
    size = SIZE[axis]
    half = size // 2
    cut = piece.shape[0] // 2
    got = {0: piece}
    down = up = piece
    for k in range(1, half):
        down = send(down, axis, -1)
        up = send(up, axis, 1)
        got[k], got[size - k] = down, up
    first = send(down[:cut], axis, -1)
    second = send(up[cut:], axis, 1)
    return [got[k] for k in range(half)] + [first, second] + [got[k] for k in range(half + 1, size)]


def largest(value):
    return jnp.max(jnp.abs(value), axis=0, keepdims=True)


def encode(value, bound):
    power = jnp.clip(jnp.ceil(jnp.log2(jnp.maximum(bound, 1e-36))), -119, 119)
    whole = jnp.round(value * (jnp.exp2(-power) * LEVELS)).astype(jnp.int16)
    tail = jnp.broadcast_to(power.astype(jnp.int16), (TAIL, value.shape[1]))
    return jnp.concatenate([whole, tail])


def decode(message):
    bound = jnp.exp2(message[-1:].astype(f32))
    return message[:-TAIL].astype(f32) * (bound * (1 / LEVELS)), bound


def ring_sum(parts, bounds, axis):
    size = SIZE[axis]
    half = size // 2
    cut = parts[0].shape[0] // 2
    first, first_bound = decode(send(encode(parts[half][:cut], bounds[half]), axis, 1))
    second, second_bound = decode(send(encode(parts[half][cut:], bounds[half]), axis, -1))
    up, down = parts[half - 1], parts[half + 1]
    up = jnp.concatenate([up[:cut] + first, up[cut:]])
    down = jnp.concatenate([down[:cut], down[cut:] + second])
    up_bound, down_bound = bounds[half - 1] + first_bound, bounds[half + 1] + second_bound
    for k in range(half - 2, -1, -1):
        up, up_bound = decode(send(encode(up, up_bound), axis, 1))
        down, down_bound = decode(send(encode(down, down_bound), axis, -1))
        if k:
            up, up_bound = up + parts[k], up_bound + bounds[k]
            down, down_bound = down + parts[size - k], down_bound + bounds[size - k]
    return parts[0] + up + down


def gather_rows(panel):
    tile = panel.shape[0] // 2
    one = jnp.concatenate(ring_gather(panel[:tile], "z"))
    two = jnp.concatenate(ring_gather(panel[tile:], "y"))
    return ring_gather(one, "y") + ring_gather(two, "z")


def cut_up(values, bounds, count):
    values = values.reshape(count, -1, values.shape[-1])
    bounds = jnp.max(bounds.reshape(count, -1, bounds.shape[-1]), axis=1, keepdims=True)
    return [values[i] for i in range(count)], [bounds[i] for i in range(count)]


def block_bounds(value, tile):
    return jnp.max(jnp.abs(value.reshape(-1, tile, value.shape[1])), axis=1)


def sum_rows(shares, bounds, tile):
    count = shares.shape[0] // 2
    blocks = count // tile
    one = ring_sum(*cut_up(shares[:count], bounds[:blocks], 4), "y")
    two = ring_sum(*cut_up(shares[count:], bounds[blocks:], 8), "z")
    one = ring_sum(*cut_up(one, block_bounds(one, tile), 8), "z")
    two = ring_sum(*cut_up(two, block_bounds(two, tile), 4), "y")
    return jnp.concatenate([one, two])


def gather_cols(panel):
    near = jnp.concatenate(ring_gather(panel, "x"))
    return [near, send(near, "core", 1)]


def sum_cols(shares, tile):
    half = shares.shape[0] // 2
    both = shares[:half] + send(shares[half:], "core", 1)
    return ring_sum(*cut_up(both, block_bounds(both, tile), 4), "x")


def sum_direct(value, axis):
    size = SIZE[axis]
    moved = [send(value, axis, k if k <= size // 2 else k - size) for k in range(1, size)]
    return functools.reduce(jnp.add, moved, value)


def sum_all(gram):
    core = lax.axis_index("core")
    place = lax.axis_index("x")
    width = gram.shape[1]
    quads = gram.reshape(2, 4, -1, width)
    mine = lax.dynamic_index_in_dim(quads, core, 0, keepdims=False)
    theirs = lax.dynamic_index_in_dim(quads, 1 - core, 0, keepdims=False)
    mine = mine + send(theirs, "core", 1)

    def pick(k):
        return lax.dynamic_index_in_dim(mine, lax.rem(place + k, 4), 0, keepdims=False)

    part = pick(0) + send(pick(1), "x", 1) + send(pick(2), "x", 2) + send(pick(3), "x", -1)
    part = sum_direct(part, "y")
    part = sum_direct(part, "z")
    got = jnp.stack([part, send(part, "x", -1), send(part, "x", 2), send(part, "x", 1)])
    back = jnp.stack(
        [lax.dynamic_index_in_dim(got, lax.rem(k - place + 4, 4), 0, keepdims=False) for k in range(4)]
    )
    other = send(back, "core", 1)
    return jnp.where(core == 0, jnp.stack([back, other]), jnp.stack([other, back])).reshape(gram.shape)


def product_kernel(transpose, spans, count_ref, to_ref, from_ref, tiles_ref, *rest):
    pieces = rest[: len(spans)]
    out_ref, bound_ref, held, total, arrived = rest[len(spans) :]
    copies = [
        pltpu.make_async_copy(piece, held.at[pl.ds(start, length)], arrived.at[i])
        for i, (piece, (start, length)) in enumerate(zip(pieces, spans))
    ]
    for copy in copies:
        copy.start()
    total[...] = jnp.zeros_like(total)
    for copy in copies:
        copy.wait()
    dims = (((0,), (0,)), ((), ())) if transpose else (((1,), (0,)), ((), ()))

    def step(i, carry):
        products = []
        for j in range(GROUP):
            slot = i * GROUP + j
            products.append(
                lax.dot_general(
                    tiles_ref[slot], held[from_ref[slot]], dims, preferred_element_type=f32
                )
            )
        for j in range(GROUP):
            total[to_ref[i * GROUP + j]] += products[j]
        return carry

    lax.fori_loop(0, (count_ref[0] + GROUP - 1) // GROUP, step, 0)

    def finish(i, carry):
        out_ref[i] = total[i]
        bound_ref[i] = jnp.max(jnp.abs(total[i]), axis=0, keepdims=True)
        return carry

    lax.fori_loop(0, out_ref.shape[0], finish, 0)


def product(tiles, pieces, to, source, count, outs, transpose):
    slots, tile, _ = tiles.shape
    width = pieces[0].shape[1]
    pieces = [piece.reshape(-1, tile, width) if piece.shape[0] % tile == 0 else piece for piece in pieces]
    spans, start = [], 0
    for piece in pieces:
        spans.append((start, piece.shape[0]))
        start += piece.shape[0]
    smem = pl.BlockSpec(memory_space=pltpu.SMEM)
    vmem = pl.BlockSpec(memory_space=pltpu.VMEM)
    out, bounds = pl.pallas_call(
        functools.partial(product_kernel, transpose, tuple(spans)),
        out_shape=[
            jax.ShapeDtypeStruct((outs, tile, width), f32),
            jax.ShapeDtypeStruct((outs, 1, width), f32),
        ],
        in_specs=[smem, smem, smem, vmem] + [pl.BlockSpec(memory_space=pl.ANY)] * len(pieces),
        out_specs=[vmem, vmem],
        scratch_shapes=[
            pltpu.VMEM((start, tile, width), bf16),
            pltpu.VMEM((outs + 1, tile, width), f32),
            pltpu.SemaphoreType.DMA((len(pieces),)),
        ],
        compiler_params=pltpu.CompilerParams(vmem_limit_bytes=48 * MIB),
        cost_estimate=pl.CostEstimate(
            flops=2 * slots * tile * tile * width,
            bytes_accessed=2 * (slots * tile * tile + (start + outs) * tile * width),
            transcendentals=0,
        ),
    )(count, to, source, tiles, *pieces)
    return out.reshape(outs * tile, width), bounds.reshape(outs, width)


def gram_of(panel):
    return lax.dot_general(panel, panel, (((0,), (0,)), ((), ())), precision=highest)


def apply_factor(panel, inverse):
    return lax.dot_general(panel, inverse, (((1,), (1,)), ((), ())), precision=highest)


def factor_kernel(gram_ref, out_ref, work):
    order = gram_ref.shape[0]
    shape = (BLOCK, 128)
    row_id = lax.broadcasted_iota(jnp.int32, shape, 0)
    unit = jnp.where(row_id == lax.broadcasted_iota(jnp.int32, shape, 1), 1.0, 0.0)
    work[:, :order] = gram_ref[...]
    square = (order, order)
    work[:, order:] = jnp.where(
        lax.broadcasted_iota(jnp.int32, square, 0) == lax.broadcasted_iota(jnp.int32, square, 1), 1.0, 0.0
    )
    for low in range(0, order, BLOCK):
        group = low // 128 * 128
        left = work[low : low + BLOCK, group : group + 128]
        right = unit
        pivots = jnp.ones(shape, f32)
        for start in range(0, BLOCK, PIVOTS):
            lane = low - group + start
            columns = [
                jnp.broadcast_to(left[:, lane + m : lane + m + 1], shape) for m in range(PIVOTS)
            ]
            for m in range(PIVOTS):
                at = start + m
                column = columns[m]
                pivot = jnp.broadcast_to(column[at : at + 1], shape)
                pivots = jnp.where(row_id == at, pivot, pivots)
                weight = jnp.where(row_id > at, column * (1.0 / pivot), 0.0)
                for q in range(m + 1, PIVOTS):
                    columns[q] = columns[q] - weight * column[start + q : start + q + 1]
                left = left - weight * left[at : at + 1]
                right = right - weight * right[at : at + 1]
        root = lax.rsqrt(pivots)
        root = root * (1.5 - 0.5 * pivots * root * root)
        right = right * root
        rows = jnp.dot(
            right[:, :BLOCK], work[low : low + BLOCK, :], precision=highest, preferred_element_type=f32
        )
        out_ref[low : low + BLOCK, :] = rows[:, order:]
        if low + BLOCK < order:
            update = lax.dot_general(
                rows[:, :order], rows, (((0,), (0,)), ((), ())), precision=highest, preferred_element_type=f32
            )
            work[low + BLOCK :, :] -= update[low + BLOCK :, :]


def inverse_factor(panel):
    gram = sum_all(gram_of(panel))
    order = gram.shape[0]
    return pl.pallas_call(
        factor_kernel,
        out_shape=jax.ShapeDtypeStruct(gram.shape, f32),
        scratch_shapes=[pltpu.VMEM((order, 2 * order), f32)],
        compiler_params=pltpu.CompilerParams(vmem_limit_bytes=16 * MIB),
    )(gram)


def on_device(omega, tiles, coords):
    tile = tiles.shape[-1]
    factor = math.sqrt(omega.shape[0] * 256)
    local_tiles = tiles.reshape(tiles.shape[2], tile, tile)
    pairs = coords.reshape(coords.shape[2], 2)
    live = pairs[:, 0] >= 0
    count = jnp.sum(live.astype(jnp.int32)).reshape(1)
    my_y, my_z = lax.axis_index("y"), lax.axis_index("z")
    my_x, my_core = lax.axis_index("x"), lax.axis_index("core")

    local_row = jnp.clip(pairs[:, 0] - (my_y * 8 + my_z) * 16, 0, 15)
    keeper = local_row // 2
    row_slot = ((keeper + my_core) % 2 * 4 + (keeper // 2 - my_x + 4) % 4) * 2 + local_row % 2
    block_col = jnp.maximum(pairs[:, 1], 0)
    owner = block_col // 16
    far_y = (owner // 8 - my_y + 4) % 4
    far_z = (owner % 8 - my_z + 8) % 8
    column_slot = jnp.where(block_col % 2 == 0, far_y * 8 + far_z, 32 + far_z * 4 + far_y)
    row_to = jnp.where(live, row_slot, 16)
    column_to = jnp.where(live, column_slot, 64)

    shares, _ = product(local_tiles, gather_rows(omega), row_to, column_slot, count, 16, False)
    one = sum_cols(shares, tile)
    one_inverse = inverse_factor(one)
    shares, bounds = product(
        local_tiles, gather_cols(one.astype(bf16)), column_to, row_slot, count, 64, True
    )
    two = apply_factor(sum_rows(shares, bounds, tile), one_inverse)
    two_inverse = inverse_factor(two)
    shares, _ = product(local_tiles, gather_rows(two.astype(bf16)), row_to, column_slot, count, 16, False)
    three = apply_factor(sum_cols(shares, tile), two_inverse)
    three_inverse = inverse_factor(three)
    return (
        apply_factor(three, three_inverse) * factor,
        apply_factor(one, one_inverse) * factor,
        apply_factor(two, two_inverse) * factor,
    )


def solution(mesh):
    mesh = Mesh(mesh.devices.reshape([SIZE[name] for name in AXES]), AXES)
    rows, cols = ("y", "z"), ("x", "core")
    return jax.shard_map(
        on_device,
        mesh=mesh,
        in_specs=(P(AXES, None), P(rows, cols, None, None, None), P(rows, cols, None, None)),
        out_specs=(P(AXES, None),) * 3,
        check_vma=False,
    )
```

```python
import functools
import math

import jax
import jax.numpy as jnp
from jax import lax
from jax.experimental import pallas as pl
from jax.experimental.pallas import tpu as pltpu
from jax.sharding import Mesh, PartitionSpec as P

highest = lax.Precision.HIGHEST
f32 = jnp.float32
bf16 = jnp.bfloat16
AXES = ("y", "z", "x", "core")
SIZE = {"y": 4, "z": 8, "x": 4, "core": 2}
GROUP = 4
BLOCK = 32
PIVOTS = 8
TAIL = 16
LEVELS = 16383.0
MIB = 1024 * 1024


def send(value, axis, step):
    size = SIZE[axis]
    return lax.ppermute(value, axis, [(i, (i + step) % size) for i in range(size)])


def ring_gather(piece, axis):
    size = SIZE[axis]
    half = size // 2
    cut = piece.shape[0] // 2
    got = {0: piece}
    down = up = piece
    for k in range(1, half):
        down = send(down, axis, -1)
        up = send(up, axis, 1)
        got[k], got[size - k] = down, up
    first = send(down[:cut], axis, -1)
    second = send(up[cut:], axis, 1)
    return [got[k] for k in range(half)] + [first, second] + [got[k] for k in range(half + 1, size)]


def largest(value):
    return jnp.max(jnp.abs(value), axis=0, keepdims=True)


def encode(value, bound):
    power = jnp.clip(jnp.ceil(jnp.log2(jnp.maximum(bound, 1e-36))), -119, 119)
    whole = jnp.round(value * (jnp.exp2(-power) * LEVELS)).astype(jnp.int16)
    tail = jnp.broadcast_to(power.astype(jnp.int16), (TAIL, value.shape[1]))
    return jnp.concatenate([whole, tail])


def decode(message):
    bound = jnp.exp2(message[-1:].astype(f32))
    return message[:-TAIL].astype(f32) * (bound * (1 / LEVELS)), bound


def largest(value):
    return jnp.max(jnp.abs(value), axis=0, keepdims=True)


def power_of(bound):
    power = jnp.clip(jnp.ceil(jnp.log2(jnp.maximum(bound, 1e-36))), -119, 119)
    return power, jnp.exp2(-power) * LEVELS


def encode(value, bound):
    power, scale = power_of(bound)
    whole = jnp.round(value * scale).astype(jnp.int16)
    tail = jnp.broadcast_to(power.astype(jnp.int16), (TAIL, value.shape[1]))
    return jnp.concatenate([whole, tail])


def decode(message):
    bound = jnp.exp2(message[-1:].astype(f32))
    return message[:-TAIL].astype(f32) * (bound * (1 / LEVELS)), bound


def ring_sum(parts, bounds, far, axis):
    size = SIZE[axis]
    half = size // 2
    cut = parts[0].shape[0] // 2
    first, first_bound = decode(send(far[0], axis, 1))
    second, second_bound = decode(send(far[1], axis, -1))
    up, down = parts[half - 1], parts[half + 1]
    up = jnp.concatenate([up[:cut] + first, up[cut:]])
    down = jnp.concatenate([down[:cut], down[cut:] + second])
    up_bound, down_bound = bounds[half - 1] + first_bound, bounds[half + 1] + second_bound
    for k in range(half - 2, -1, -1):
        up, up_bound = decode(send(encode(up, up_bound), axis, 1))
        down, down_bound = decode(send(encode(down, down_bound), axis, -1))
        if k:
            up, up_bound = up + parts[k], up_bound + bounds[k]
            down, down_bound = down + parts[size - k], down_bound + bounds[size - k]
    return parts[0] + up + down


def direct_gather(piece, axis):
    size = SIZE[axis]
    return [piece] + [send(piece, axis, -k if k <= size // 2 else size - k) for k in range(1, size)]


def gather_rows(panel):
    tile = panel.shape[0] // 2
    two = jnp.concatenate(direct_gather(panel[tile:], "y"))
    one = jnp.broadcast_to(panel[:tile], (8, tile, panel.shape[1])).reshape(8 * tile, -1)
    one = lax.all_to_all(one, "z", split_axis=0, concat_axis=0, tiled=True)
    return ring_gather(one, "y") + ring_gather(two, "z")


def sum_rows(shares):
    near, near_bound, up, up_bound, down, down_bound, *far = shares
    total = ring_sum([near, up, None, down], [near_bound, up_bound, None, down_bound], far, "y")
    parts = total.reshape(8, -1, total.shape[1])
    messages = jnp.concatenate([encode(parts[k], largest(parts[k]))[None] for k in range(8)])
    rows = messages.shape[1]
    messages = lax.all_to_all(messages.reshape(8 * rows, -1), "z", split_axis=0, concat_axis=0, tiled=True)
    messages = messages.reshape(8, rows, -1)
    return sum(decode(messages[k])[0] for k in range(8))


def gather_cols(panel):
    near = jnp.concatenate(ring_gather(panel, "x"))
    return [near, send(near, "core", 1)]


def sum_cols(shares):
    near, _, far, _ = shares
    both = (near + send(far, "core", 1)).reshape(4, -1, near.shape[1])
    total = both[0]
    for k in range(1, 4):
        message = encode(both[k], largest(both[k]))
        total = total + decode(send(message, "x", k if k < 3 else -1))[0]
    return total


def sum_direct(value, axis):
    size = SIZE[axis]
    moved = [send(value, axis, k if k <= size // 2 else k - size) for k in range(1, size)]
    return functools.reduce(jnp.add, moved, value)


def sum_all(gram):
    core = lax.axis_index("core")
    place = lax.axis_index("x")
    width = gram.shape[1]
    quads = gram.reshape(2, 4, -1, width)
    mine = lax.dynamic_index_in_dim(quads, core, 0, keepdims=False)
    theirs = lax.dynamic_index_in_dim(quads, 1 - core, 0, keepdims=False)
    mine = mine + send(theirs, "core", 1)

    def pick(k):
        return lax.dynamic_index_in_dim(mine, lax.rem(place + k, 4), 0, keepdims=False)

    part = pick(0) + send(pick(1), "x", 1) + send(pick(2), "x", 2) + send(pick(3), "x", -1)
    part = sum_direct(part, "y")
    part = sum_direct(part, "z")
    got = jnp.stack([part, send(part, "x", -1), send(part, "x", 2), send(part, "x", 1)])
    back = jnp.stack(
        [lax.dynamic_index_in_dim(got, lax.rem(k - place + 4, 4), 0, keepdims=False) for k in range(4)]
    )
    other = send(back, "core", 1)
    return jnp.where(core == 0, jnp.stack([back, other]), jnp.stack([other, back])).reshape(gram.shape)


def sum_over_cols(gram):
    core = lax.axis_index("core")
    halves = gram.reshape(2, -1, gram.shape[1])
    mine = lax.dynamic_index_in_dim(halves, core, 0, keepdims=False)
    theirs = lax.dynamic_index_in_dim(halves, 1 - core, 0, keepdims=False)
    mine = sum_direct(mine + send(theirs, "core", 1), "x")
    other = send(mine, "core", 1)
    return jnp.where(core == 0, jnp.stack([mine, other]), jnp.stack([other, mine])).reshape(gram.shape)


def product_kernel(transpose, spans, plain, coded, with_gram, count_ref, to_ref, from_ref, tiles_ref, *rest):
    pieces, rest = rest[: len(spans)], rest[len(spans) :]
    outs, rest = rest[: 2 * len(plain) + len(coded) + with_gram], rest[2 * len(plain) + len(coded) + with_gram :]
    held, total, arrived = rest
    copies = [
        pltpu.make_async_copy(piece, held.at[pl.ds(start, length)], arrived.at[i])
        for i, (piece, (start, length)) in enumerate(zip(pieces, spans))
    ]
    for copy in copies:
        copy.start()
    total[...] = jnp.zeros_like(total)
    for copy in copies:
        copy.wait()
    dims = (((0,), (0,)), ((), ())) if transpose else (((1,), (0,)), ((), ()))

    def step(i, carry):
        products = []
        for j in range(GROUP):
            slot = i * GROUP + j
            products.append(
                lax.dot_general(tiles_ref[slot], held[from_ref[slot]], dims, preferred_element_type=f32)
            )
        for j in range(GROUP):
            total[to_ref[i * GROUP + j]] += products[j]
        return carry

    lax.fori_loop(0, (count_ref[0] + GROUP - 1) // GROUP, step, 0)

    def bound_of(start, blocks):
        def widen(i, bound):
            return jnp.maximum(bound, jnp.max(jnp.abs(total[start + i]), axis=0, keepdims=True))

        return lax.fori_loop(0, blocks, widen, jnp.zeros((1, total.shape[2]), f32))

    start = 0
    for k, blocks in enumerate(plain):
        out_ref, bound_ref = outs[2 * k], outs[2 * k + 1]

        def finish(i, carry, out_ref=out_ref, start=start):
            out_ref[i] = total[start + i]
            return carry

        lax.fori_loop(0, blocks, finish, 0)
        bound_ref[...] = bound_of(start, blocks)
        start += blocks
    tile = total.shape[1]
    for k, blocks in enumerate(coded):
        out_ref = outs[2 * len(plain) + k]
        power, scale = power_of(bound_of(start, blocks))

        def finish(i, carry, out_ref=out_ref, start=start, scale=scale):
            rows = pl.ds(pl.multiple_of(i * tile, tile), tile)
            out_ref[rows, :] = jnp.round(total[start + i] * scale).astype(jnp.int32).astype(jnp.int16)
            return carry

        lax.fori_loop(0, blocks, finish, 0)
        out_ref[blocks * tile :, :] = jnp.broadcast_to(power, (TAIL, power.shape[1])).astype(jnp.int32).astype(jnp.int16)
        start += blocks
    if with_gram:
        gram_ref = outs[-1]
        gram_ref[...] = jnp.zeros_like(gram_ref)

        def add(i, carry):
            block = held[pl.ds(i * GROUP, GROUP)].reshape(GROUP * tile, -1)
            gram_ref[...] += lax.dot_general(block, block, (((0,), (0,)), ((), ())), preferred_element_type=f32)
            return carry

        lax.fori_loop(0, held.shape[0] // GROUP, add, 0)


def product(tiles, pieces, to, source, count, plain, coded, transpose, with_gram=False):
    slots, tile, _ = tiles.shape
    width = pieces[0].shape[1]
    pieces = [piece.reshape(-1, tile, width) for piece in pieces]
    spans, start = [], 0
    for piece in pieces:
        spans.append((start, piece.shape[0]))
        start += piece.shape[0]
    outs = sum(plain) + sum(coded)
    smem = pl.BlockSpec(memory_space=pltpu.SMEM)
    vmem = pl.BlockSpec(memory_space=pltpu.VMEM)
    shapes = []
    for blocks in plain:
        shapes += [jax.ShapeDtypeStruct((blocks, tile, width), f32), jax.ShapeDtypeStruct((1, width), f32)]
    shapes += [jax.ShapeDtypeStruct((blocks * tile + TAIL, width), jnp.int16) for blocks in coded]
    shapes += [jax.ShapeDtypeStruct((width, width), f32)] * with_gram
    found = pl.pallas_call(
        functools.partial(product_kernel, transpose, tuple(spans), plain, coded, with_gram),
        out_shape=shapes,
        in_specs=[smem, smem, smem, vmem] + [pl.BlockSpec(memory_space=pl.ANY)] * len(pieces),
        out_specs=[vmem] * len(shapes),
        scratch_shapes=[
            pltpu.VMEM((start, tile, width), bf16),
            pltpu.VMEM((outs + 1, tile, width), f32),
            pltpu.SemaphoreType.DMA((len(pieces),)),
        ],
        compiler_params=pltpu.CompilerParams(vmem_limit_bytes=48 * MIB),
        cost_estimate=pl.CostEstimate(
            flops=2 * slots * tile * tile * width,
            bytes_accessed=2 * (slots * tile * tile + (start + 2 * outs) * tile * width),
            transcendentals=0,
        ),
    )(count, to, source, tiles, *pieces)
    return [x.reshape(-1, width) for x in found]


def gram_of(panel):
    return lax.dot_general(panel, panel, (((0,), (0,)), ((), ())), precision=highest)


def apply_factor(panel, inverse):
    return lax.dot_general(panel, inverse, (((1,), (1,)), ((), ())), precision=highest)


def factor_kernel(gram_ref, out_ref, work):
    order = gram_ref.shape[0]
    shape = (BLOCK, 128)
    row_id = lax.broadcasted_iota(jnp.int32, shape, 0)
    unit = jnp.where(row_id == lax.broadcasted_iota(jnp.int32, shape, 1), 1.0, 0.0)
    work[:, :order] = gram_ref[...]
    square = (order, order)
    work[:, order:] = jnp.where(
        lax.broadcasted_iota(jnp.int32, square, 0) == lax.broadcasted_iota(jnp.int32, square, 1), 1.0, 0.0
    )
    for low in range(0, order, BLOCK):
        group = low // 128 * 128
        left = work[low : low + BLOCK, group : group + 128]
        right = unit
        pivots = jnp.ones(shape, f32)
        for start in range(0, BLOCK, PIVOTS):
            lane = low - group + start
            columns = [
                jnp.broadcast_to(left[:, lane + m : lane + m + 1], shape) for m in range(PIVOTS)
            ]
            for m in range(PIVOTS):
                at = start + m
                column = columns[m]
                pivot = jnp.broadcast_to(column[at : at + 1], shape)
                pivots = jnp.where(row_id == at, pivot, pivots)
                weight = jnp.where(row_id > at, column * (1.0 / pivot), 0.0)
                for q in range(m + 1, PIVOTS):
                    columns[q] = columns[q] - weight * column[start + q : start + q + 1]
                left = left - weight * left[at : at + 1]
                right = right - weight * right[at : at + 1]
        root = lax.rsqrt(pivots)
        root = root * (1.5 - 0.5 * pivots * root * root)
        right = right * root
        rows = jnp.dot(
            right[:, :BLOCK], work[low : low + BLOCK, :], precision=highest, preferred_element_type=f32
        )
        out_ref[low : low + BLOCK, :] = rows[:, order:]
        if low + BLOCK < order:
            update = lax.dot_general(
                rows[:, :order], rows, (((0,), (0,)), ((), ())), precision=highest, preferred_element_type=f32
            )
            work[low + BLOCK :, :] -= update[low + BLOCK :, :]


def inverse_factor(gram):
    order = gram.shape[0]
    return pl.pallas_call(
        factor_kernel,
        out_shape=jax.ShapeDtypeStruct(gram.shape, f32),
        scratch_shapes=[pltpu.VMEM((order, 2 * order), f32)],
        compiler_params=pltpu.CompilerParams(vmem_limit_bytes=16 * MIB),
    )(gram)


def on_device(omega, tiles, coords):
    tile = tiles.shape[-1]
    factor = math.sqrt(omega.shape[0] * 256)
    local_tiles = tiles.reshape(tiles.shape[2], tile, tile)
    pairs = coords.reshape(coords.shape[2], 2)
    live = pairs[:, 0] >= 0
    count = jnp.sum(live.astype(jnp.int32)).reshape(1)
    my_y, my_z = lax.axis_index("y"), lax.axis_index("z")
    my_x, my_core = lax.axis_index("x"), lax.axis_index("core")

    local_row = jnp.clip(pairs[:, 0] - (my_y * 8 + my_z) * 16, 0, 15)
    keeper = local_row // 2
    row_slot = ((keeper + my_core) % 2 * 4 + (keeper // 2 - my_x + 4) % 4) * 2 + local_row % 2
    block_col = jnp.maximum(pairs[:, 1], 0)
    owner = block_col // 16
    far_y = (owner // 8 - my_y + 4) % 4
    far_z = (owner % 8 - my_z + 8) % 8
    panel_slot = jnp.where(block_col % 2 == 0, far_y * 8 + owner % 8, 32 + far_z * 4 + far_y)
    order_y = jnp.where(far_y == 2, 3, jnp.where(far_y == 3, 2, far_y))
    column_slot = (order_y * 8 + owner % 8) * 2 + block_col % 2
    row_to = jnp.where(live, row_slot, 16)
    column_to = jnp.where(live, column_slot, 64)

    def forward(panel, with_gram=False):
        pieces = gather_rows(panel.astype(bf16))
        return product(local_tiles, pieces, row_to, panel_slot, count, (8, 8), (), False, with_gram)

    one = sum_cols(forward(omega))
    shares = product(
        local_tiles, gather_cols(one.astype(bf16)), column_to, row_slot, count, (16, 16, 16), (8, 8), True
    )
    held_back = lax.optimization_barrier((one, shares[1]))[0]
    one_inverse = inverse_factor(sum_all(gram_of(held_back)))
    two = apply_factor(sum_rows(shares), one_inverse)
    *shares, gram = forward(two, True)
    two_inverse = inverse_factor(sum_over_cols(gram))
    three = apply_factor(sum_cols(shares), two_inverse)
    three_inverse = inverse_factor(sum_all(gram_of(three)))
    return (
        apply_factor(three, three_inverse) * factor,
        apply_factor(one, one_inverse) * factor,
        apply_factor(two, two_inverse) * factor,
    )


def solution(mesh):
    mesh = Mesh(mesh.devices.reshape([SIZE[name] for name in AXES]), AXES)
    rows, cols = ("y", "z"), ("x", "core")
    return jax.shard_map(
        on_device,
        mesh=mesh,
        in_specs=(P(AXES, None), P(rows, cols, None, None, None), P(rows, cols, None, None)),
        out_specs=(P(AXES, None),) * 3,
        check_vma=False,
    )
```

```python
import functools
import math

import jax
import jax.numpy as jnp
from jax import lax
from jax.experimental import pallas as pl
from jax.experimental.pallas import tpu as pltpu
from jax.sharding import Mesh, PartitionSpec as P

highest = lax.Precision.HIGHEST
f32 = jnp.float32
bf16 = jnp.bfloat16
AXES = ("y", "z", "x", "core")
SIZE = {"y": 4, "z": 8, "x": 4, "core": 2}
GROUP = 4
BLOCK = 32
PIVOTS = 8
TAIL = 16
LEVELS = 16383.0
MIB = 1024 * 1024
GIGA = 1000**3


def send(value, axis, step):
    size = SIZE[axis]
    return lax.ppermute(value, axis, [(i, (i + step) % size) for i in range(size)])


def ring_gather(piece, axis):
    size = SIZE[axis]
    half = size // 2
    cut = piece.shape[0] // 2
    got = {0: piece}
    down = up = piece
    for k in range(1, half):
        down = send(down, axis, -1)
        up = send(up, axis, 1)
        got[k], got[size - k] = down, up
    first = send(down[:cut], axis, -1)
    second = send(up[cut:], axis, 1)
    return [got[k] for k in range(half)] + [first, second] + [got[k] for k in range(half + 1, size)]


def largest(value):
    return jnp.max(jnp.abs(value), axis=-2, keepdims=True)


def power_of(bound):
    power = jnp.clip(jnp.ceil(jnp.log2(jnp.maximum(bound, 1e-36))), -119, 119)
    return power, jnp.exp2(-power) * LEVELS


def encode(value, bound):
    power, scale = power_of(bound)
    whole = jnp.round(value * scale).astype(jnp.int16)
    tail = jnp.broadcast_to(power.astype(jnp.int16), value.shape[:-2] + (TAIL, value.shape[-1]))
    return jnp.concatenate([whole, tail], axis=-2)


def decode(message):
    bound = jnp.exp2(message[..., -1:, :].astype(f32))
    return message[..., :-TAIL, :].astype(f32) * (bound * (1 / LEVELS)), bound


def together(*values):
    return lax.optimization_barrier(values)


def direct_gather(piece, axis):
    size = SIZE[axis]
    return [piece] + [send(piece, axis, -k if k <= size // 2 else size - k) for k in range(1, size)]


def gather_rows(panel):
    tile = panel.shape[0] // 2
    two = jnp.concatenate(direct_gather(panel[tile:], "y"))
    one = jnp.broadcast_to(panel[:tile], (8, tile, panel.shape[1])).reshape(8 * tile, -1)
    one = lax.all_to_all(one, "z", split_axis=0, concat_axis=0, tiled=True)
    return ring_gather(one, "y") + ring_gather(two, "z")


def sum_rows(shares, gram):
    near, _, up, up_bound, down, down_bound, *far = shares
    cut = near.shape[0] // 2
    first, second = send(far[0], "y", 1), send(far[1], "y", -1)
    gram = gram_near(gram)
    first, second, gram = together(first, second, gram)
    first, first_bound = decode(first)
    second, second_bound = decode(second)
    up = jnp.concatenate([up[:cut] + first, up[cut:]])
    down = jnp.concatenate([down[:cut], down[cut:] + second])
    up = send(encode(up, up_bound + first_bound), "y", 1)
    down = send(encode(down, down_bound + second_bound), "y", -1)
    gram = gram_far(gram)
    up, down, gram = together(up, down, gram)
    total = (near + decode(up)[0] + decode(down)[0]).reshape(8, -1, near.shape[1])
    messages = encode(total, largest(total))
    rows = messages.shape[1]
    messages = lax.all_to_all(messages.reshape(8 * rows, -1), "z", split_axis=0, concat_axis=0, tiled=True)
    inverse = inverse_factor(gram_back(gram))
    messages, inverse = together(messages, inverse)
    return jnp.sum(decode(messages.reshape(8, rows, -1))[0], axis=0), inverse


def gather_cols(panel):
    near = jnp.concatenate(ring_gather(panel, "x"))
    return [near, send(near, "core", 1)]


def sum_cols(shares):
    near, _, far, _ = shares
    both = (near + send(far, "core", 1)).reshape(4, -1, near.shape[1])
    messages = encode(both, largest(both))
    moved = [send(messages[k], "x", k if k < 3 else -1) for k in range(1, 4)]
    return functools.reduce(jnp.add, [decode(message)[0] for message in moved], both[0])


def sum_direct(value, axis):
    size = SIZE[axis]
    moved = [send(value, axis, k if k <= size // 2 else k - size) for k in range(1, size)]
    return functools.reduce(jnp.add, moved, value)


def sum_flipped(value, axis, flips):
    moved = [lax.ppermute(value, axis, [(i, i ^ flip) for i in range(SIZE[axis])]) for flip in flips]
    return functools.reduce(jnp.add, moved, value)


def gram_near(gram):
    core = lax.axis_index("core")
    place = lax.axis_index("x")
    quads = gram.reshape(2, 4, -1, gram.shape[1])
    mine = lax.dynamic_index_in_dim(quads, core, 0, keepdims=False)
    theirs = lax.dynamic_index_in_dim(quads, 1 - core, 0, keepdims=False)
    mine = mine + send(theirs, "core", 1)

    def pick(k):
        return lax.dynamic_index_in_dim(mine, lax.rem(place + k, 4), 0, keepdims=False)

    return pick(0) + send(pick(1), "x", 1) + send(pick(2), "x", 2) + send(pick(3), "x", -1)


def gram_far(part):
    return sum_flipped(sum_flipped(sum_direct(part, "y"), "z", (1, 2, 3)), "z", (4,))


def gram_back(part):
    core = lax.axis_index("core")
    place = lax.axis_index("x")
    got = jnp.stack([part, send(part, "x", -1), send(part, "x", 2), send(part, "x", 1)])
    back = jnp.stack(
        [lax.dynamic_index_in_dim(got, lax.rem(k - place + 4, 4), 0, keepdims=False) for k in range(4)]
    )
    other = send(back, "core", 1)
    both = jnp.where(core == 0, jnp.stack([back, other]), jnp.stack([other, back]))
    return both.reshape(-1, part.shape[1])


def sum_over_cols(gram):
    core = lax.axis_index("core")
    halves = gram.reshape(2, -1, gram.shape[1])
    mine = lax.dynamic_index_in_dim(halves, core, 0, keepdims=False)
    theirs = lax.dynamic_index_in_dim(halves, 1 - core, 0, keepdims=False)
    mine = sum_direct(mine + send(theirs, "core", 1), "x")
    other = send(mine, "core", 1)
    return jnp.where(core == 0, jnp.stack([mine, other]), jnp.stack([other, mine])).reshape(gram.shape)


def product_kernel(transpose, spans, plain, coded, with_gram, count_ref, to_ref, from_ref, tiles_ref, *rest):
    pieces, rest = rest[: len(spans)], rest[len(spans) :]
    outs, rest = rest[: 2 * len(plain) + len(coded) + with_gram], rest[2 * len(plain) + len(coded) + with_gram :]
    held, total, arrived = rest
    copies = [
        pltpu.make_async_copy(piece, held.at[pl.ds(start, length)], arrived.at[i])
        for i, (piece, (start, length)) in enumerate(zip(pieces, spans))
    ]
    for copy in copies:
        copy.start()
    total[...] = jnp.zeros_like(total)
    for copy in copies:
        copy.wait()
    dims = (((0,), (0,)), ((), ())) if transpose else (((1,), (0,)), ((), ()))

    def step(i, carry):
        products = []
        for j in range(GROUP):
            slot = i * GROUP + j
            products.append(
                lax.dot_general(tiles_ref[slot], held[from_ref[slot]], dims, preferred_element_type=f32)
            )
        for j in range(GROUP):
            total[to_ref[i * GROUP + j]] += products[j]
        return carry

    lax.fori_loop(0, (count_ref[0] + GROUP - 1) // GROUP, step, 0)

    def bound_of(start, blocks):
        def widen(i, bound):
            return jnp.maximum(bound, jnp.max(jnp.abs(total[start + i]), axis=0, keepdims=True))

        return lax.fori_loop(0, blocks, widen, jnp.zeros((1, total.shape[2]), f32))

    start = 0
    for k, blocks in enumerate(plain):
        out_ref, bound_ref = outs[2 * k], outs[2 * k + 1]

        def finish(i, carry, out_ref=out_ref, start=start):
            out_ref[i] = total[start + i]
            return carry

        lax.fori_loop(0, blocks, finish, 0)
        bound_ref[...] = bound_of(start, blocks)
        start += blocks
    tile = total.shape[1]
    for k, blocks in enumerate(coded):
        out_ref = outs[2 * len(plain) + k]
        power, scale = power_of(bound_of(start, blocks))

        def finish(i, carry, out_ref=out_ref, start=start, scale=scale):
            rows = pl.ds(pl.multiple_of(i * tile, tile), tile)
            out_ref[rows, :] = jnp.round(total[start + i] * scale).astype(jnp.int32).astype(jnp.int16)
            return carry

        lax.fori_loop(0, blocks, finish, 0)
        out_ref[blocks * tile :, :] = jnp.broadcast_to(power, (TAIL, power.shape[1])).astype(jnp.int32).astype(jnp.int16)
        start += blocks
    if with_gram:
        gram_ref = outs[-1]
        gram_ref[...] = jnp.zeros_like(gram_ref)

        def add(i, carry):
            block = held[pl.ds(i * GROUP, GROUP)].reshape(GROUP * tile, -1)
            gram_ref[...] += lax.dot_general(block, block, (((0,), (0,)), ((), ())), preferred_element_type=f32)
            return carry

        lax.fori_loop(0, held.shape[0] // GROUP, add, 0)


def product(tiles, pieces, to, source, count, plain, coded, transpose, with_gram=False):
    slots, tile, _ = tiles.shape
    width = pieces[0].shape[1]
    pieces = [piece.reshape(-1, tile, width) for piece in pieces]
    spans, start = [], 0
    for piece in pieces:
        spans.append((start, piece.shape[0]))
        start += piece.shape[0]
    outs = sum(plain) + sum(coded)
    smem = pl.BlockSpec(memory_space=pltpu.SMEM)
    vmem = pl.BlockSpec(memory_space=pltpu.VMEM)
    shapes = []
    for blocks in plain:
        shapes += [jax.ShapeDtypeStruct((blocks, tile, width), f32), jax.ShapeDtypeStruct((1, width), f32)]
    shapes += [jax.ShapeDtypeStruct((blocks * tile + TAIL, width), jnp.int16) for blocks in coded]
    shapes += [jax.ShapeDtypeStruct((width, width), f32)] * with_gram
    found = pl.pallas_call(
        functools.partial(product_kernel, transpose, tuple(spans), plain, coded, with_gram),
        out_shape=shapes,
        in_specs=[smem, smem, smem, vmem] + [pl.BlockSpec(memory_space=pl.ANY)] * len(pieces),
        out_specs=[vmem] * len(shapes),
        scratch_shapes=[
            pltpu.VMEM((start, tile, width), bf16),
            pltpu.VMEM((outs + 1, tile, width), f32),
            pltpu.SemaphoreType.DMA((len(pieces),)),
        ],
        compiler_params=pltpu.CompilerParams(vmem_limit_bytes=48 * MIB),
        cost_estimate=pl.CostEstimate(
            flops=2 * slots * tile * tile * width,
            bytes_accessed=2 * (slots * tile * tile + (start + 2 * outs) * tile * width),
            transcendentals=0,
        ),
    )(count, to, source, tiles, *pieces)
    return [x.reshape(-1, width) for x in found]


def gram_of(panel):
    return lax.dot_general(panel, panel, (((0,), (0,)), ((), ())), precision=highest)


def apply_factor(panel, inverse):
    return lax.dot_general(panel, inverse, (((1,), (1,)), ((), ())), precision=highest)


def factor_kernel(gram_ref, out_ref, work):
    order = gram_ref.shape[0]
    shape = (BLOCK, 128)
    row_id = lax.broadcasted_iota(jnp.int32, shape, 0)
    unit = jnp.where(row_id == lax.broadcasted_iota(jnp.int32, shape, 1), 1.0, 0.0)
    work[:, :order] = gram_ref[...]
    square = (order, order)
    work[:, order:] = jnp.where(
        lax.broadcasted_iota(jnp.int32, square, 0) == lax.broadcasted_iota(jnp.int32, square, 1), 1.0, 0.0
    )
    for low in range(0, order, BLOCK):
        group = low // 128 * 128
        left = work[low : low + BLOCK, group : group + 128]
        right = unit
        pivots = jnp.ones(shape, f32)
        for start in range(0, BLOCK, PIVOTS):
            lane = low - group + start
            columns = [
                jnp.broadcast_to(left[:, lane + m : lane + m + 1], shape) for m in range(PIVOTS)
            ]
            for m in range(PIVOTS):
                at = start + m
                column = columns[m]
                pivot = jnp.broadcast_to(column[at : at + 1], shape)
                pivots = jnp.where(row_id == at, pivot, pivots)
                weight = jnp.where(row_id > at, column * (1.0 / pivot), 0.0)
                for q in range(m + 1, PIVOTS):
                    columns[q] = columns[q] - weight * column[start + q : start + q + 1]
                left = left - weight * left[at : at + 1]
                right = right - weight * right[at : at + 1]
        root = lax.rsqrt(pivots)
        root = root * (1.5 - 0.5 * pivots * root * root)
        right = right * root
        rows = jnp.dot(
            right[:, :BLOCK], work[low : low + BLOCK, :], precision=highest, preferred_element_type=f32
        )
        out_ref[low : low + BLOCK, :] = rows[:, order:]
        if low + BLOCK < order:
            update = lax.dot_general(
                rows[:, :order], rows, (((0,), (0,)), ((), ())), precision=highest, preferred_element_type=f32
            )
            work[low + BLOCK :, :] -= update[low + BLOCK :, :]


def inverse_factor(gram):
    order = gram.shape[0]
    return pl.pallas_call(
        factor_kernel,
        out_shape=jax.ShapeDtypeStruct(gram.shape, f32),
        scratch_shapes=[pltpu.VMEM((order, 2 * order), f32)],
        compiler_params=pltpu.CompilerParams(vmem_limit_bytes=16 * MIB),
        cost_estimate=pl.CostEstimate(flops=12 * GIGA, bytes_accessed=40 * MIB, transcendentals=0),
    )(gram)


def on_device(omega, tiles, coords):
    tile = tiles.shape[-1]
    factor = math.sqrt(omega.shape[0] * 256)
    local_tiles = tiles.reshape(tiles.shape[2], tile, tile)
    pairs = coords.reshape(coords.shape[2], 2)
    live = pairs[:, 0] >= 0
    count = jnp.sum(live.astype(jnp.int32)).reshape(1)
    my_y, my_z = lax.axis_index("y"), lax.axis_index("z")
    my_x, my_core = lax.axis_index("x"), lax.axis_index("core")

    local_row = jnp.clip(pairs[:, 0] - (my_y * 8 + my_z) * 16, 0, 15)
    keeper = local_row // 2
    row_slot = ((keeper + my_core) % 2 * 4 + (keeper // 2 - my_x + 4) % 4) * 2 + local_row % 2
    block_col = jnp.maximum(pairs[:, 1], 0)
    owner = block_col // 16
    far_y = (owner // 8 - my_y + 4) % 4
    far_z = (owner % 8 - my_z + 8) % 8
    panel_slot = jnp.where(block_col % 2 == 0, far_y * 8 + owner % 8, 32 + far_z * 4 + far_y)
    order_y = jnp.where(far_y == 2, 3, jnp.where(far_y == 3, 2, far_y))
    column_slot = (order_y * 8 + owner % 8) * 2 + block_col % 2
    row_to = jnp.where(live, row_slot, 16)
    column_to = jnp.where(live, column_slot, 64)

    def forward(panel, with_gram=False):
        pieces = gather_rows(panel.astype(bf16))
        return product(local_tiles, pieces, row_to, panel_slot, count, (8, 8), (), False, with_gram)

    one = sum_cols(forward(omega))
    shares = product(
        local_tiles, gather_cols(one.astype(bf16)), column_to, row_slot, count, (16, 16, 16), (8, 8), True
    )
    held_back, *shares = together(one, *shares)
    total, one_inverse = sum_rows(shares, gram_of(held_back))
    two = apply_factor(total, one_inverse)
    *shares, gram = forward(two, True)
    two_inverse = inverse_factor(sum_over_cols(gram))
    three = apply_factor(sum_cols(shares), two_inverse)
    three_inverse = inverse_factor(gram_back(gram_far(gram_near(gram_of(three)))))
    return (
        apply_factor(three, three_inverse) * factor,
        apply_factor(one, one_inverse) * factor,
        apply_factor(two, two_inverse) * factor,
    )


def solution(mesh):
    mesh = Mesh(mesh.devices.reshape([SIZE[name] for name in AXES]), AXES)
    rows, cols = ("y", "z"), ("x", "core")
    return jax.shard_map(
        on_device,
        mesh=mesh,
        in_specs=(P(AXES, None), P(rows, cols, None, None, None), P(rows, cols, None, None)),
        out_specs=(P(AXES, None),) * 3,
        check_vma=False,
    )
```

```python
import functools
import math

import jax
import jax.numpy as jnp
from jax import lax
from jax.experimental import pallas as pl
from jax.experimental.pallas import tpu as pltpu
from jax.sharding import Mesh, PartitionSpec as P

highest = lax.Precision.HIGHEST
f32 = jnp.float32
bf16 = jnp.bfloat16
AXES = ("y", "z", "x", "core")
SIZE = {"y": 4, "z": 8, "x": 4, "core": 2}
GROUP = 4
BLOCK = 64
PIVOTS = 16
TAIL = 16
LEVELS = 16383.0
MIB = 1024 * 1024
GIGA = 1000**3


def send(value, axis, step):
    size = SIZE[axis]
    return lax.ppermute(value, axis, [(i, (i + step) % size) for i in range(size)])


def ring_gather(piece, axis):
    size = SIZE[axis]
    half = size // 2
    cut = piece.shape[0] // 2
    got = {0: piece}
    down = up = piece
    for k in range(1, half):
        down = send(down, axis, -1)
        up = send(up, axis, 1)
        got[k], got[size - k] = down, up
    first = send(down[:cut], axis, -1)
    second = send(up[cut:], axis, 1)
    return [got[k] for k in range(half)] + [first, second] + [got[k] for k in range(half + 1, size)]


def largest(value):
    return jnp.max(jnp.abs(value), axis=-2, keepdims=True)


def power_of(bound):
    power = jnp.clip(jnp.ceil(jnp.log2(jnp.maximum(bound, 1e-36))), -119, 119)
    return power, jnp.exp2(-power) * LEVELS


def encode(value, bound):
    power, scale = power_of(bound)
    whole = jnp.round(value * scale).astype(jnp.int16)
    tail = jnp.broadcast_to(power.astype(jnp.int16), value.shape[:-2] + (TAIL, value.shape[-1]))
    return jnp.concatenate([whole, tail], axis=-2)


def decode(message):
    bound = jnp.exp2(message[..., -1:, :].astype(f32))
    return message[..., :-TAIL, :].astype(f32) * (bound * (1 / LEVELS)), bound


def together(*values):
    return lax.optimization_barrier(values)


def direct_gather(piece, axis):
    size = SIZE[axis]
    return [piece] + [send(piece, axis, -k if k <= size // 2 else size - k) for k in range(1, size)]


def gather_rows(panel):
    tile = panel.shape[0] // 2
    two = jnp.concatenate(direct_gather(panel[tile:], "y"))
    one = jnp.broadcast_to(panel[:tile], (8, tile, panel.shape[1])).reshape(8 * tile, -1)
    one = lax.all_to_all(one, "z", split_axis=0, concat_axis=0, tiled=True)
    return ring_gather(one, "y") + ring_gather(two, "z")


def sum_rows(first, second, shares, gram):
    near, _, up, up_bound, down, down_bound = shares
    cut = near.shape[0] // 2
    gram = gram_near(gram)
    first, second, gram = together(first, second, gram)
    first, first_bound = decode(first)
    second, second_bound = decode(second)
    up = jnp.concatenate([up[:cut] + first, up[cut:]])
    down = jnp.concatenate([down[:cut], down[cut:] + second])
    up = send(encode(up, up_bound + first_bound), "y", 1)
    down = send(encode(down, down_bound + second_bound), "y", -1)
    gram = sum_along_z(gram)
    up, down, gram = together(up, down, gram)
    total = (near + decode(up)[0] + decode(down)[0]).reshape(8, -1, near.shape[1])
    messages = encode(total, largest(total))
    rows = messages.shape[1]
    messages = lax.all_to_all(messages.reshape(8 * rows, -1), "z", split_axis=0, concat_axis=0, tiled=True)
    inverse = inverse_factor(gram_back(sum_direct(gram, "y")))
    messages, inverse = together(messages, inverse)
    return jnp.sum(decode(messages.reshape(8, rows, -1))[0], axis=0), inverse


def gather_cols(panel):
    near = jnp.concatenate(ring_gather(panel, "x"))
    return [near, send(near, "core", 1)]


def exchange_cols(shares):
    near, _, far, _ = shares
    both = (near + send(far, "core", 1)).reshape(4, -1, near.shape[1])
    messages = encode(both, largest(both))
    return [both[0]] + [send(messages[k], "x", k if k < 3 else -1) for k in range(1, 4)]


def sum_cols(parts):
    return functools.reduce(jnp.add, [decode(message)[0] for message in parts[1:]], parts[0])


def sum_direct(value, axis):
    size = SIZE[axis]
    moved = [send(value, axis, k if k <= size // 2 else k - size) for k in range(1, size)]
    return functools.reduce(jnp.add, moved, value)


def sum_flipped(value, axis, flips):
    moved = [lax.ppermute(value, axis, [(i, i ^ flip) for i in range(SIZE[axis])]) for flip in flips]
    return functools.reduce(jnp.add, moved, value)


def gram_near(gram):
    core = lax.axis_index("core")
    place = lax.axis_index("x")
    quads = gram.reshape(2, 4, -1, gram.shape[1])
    mine = lax.dynamic_index_in_dim(quads, core, 0, keepdims=False)
    theirs = lax.dynamic_index_in_dim(quads, 1 - core, 0, keepdims=False)
    mine = mine + send(theirs, "core", 1)

    def pick(k):
        return lax.dynamic_index_in_dim(mine, lax.rem(place + k, 4), 0, keepdims=False)

    return pick(0) + send(pick(1), "x", 1) + send(pick(2), "x", 2) + send(pick(3), "x", -1)


def sum_along_z(part):
    return sum_flipped(sum_flipped(part, "z", (1, 2, 3)), "z", (4,))


def gram_back(part):
    core = lax.axis_index("core")
    place = lax.axis_index("x")
    got = jnp.stack([part, send(part, "x", -1), send(part, "x", 2), send(part, "x", 1)])
    back = jnp.stack(
        [lax.dynamic_index_in_dim(got, lax.rem(k - place + 4, 4), 0, keepdims=False) for k in range(4)]
    )
    other = send(back, "core", 1)
    both = jnp.where(core == 0, jnp.stack([back, other]), jnp.stack([other, back]))
    return both.reshape(-1, part.shape[1])


def sum_over_cols(gram):
    core = lax.axis_index("core")
    halves = gram.reshape(2, -1, gram.shape[1])
    mine = lax.dynamic_index_in_dim(halves, core, 0, keepdims=False)
    theirs = lax.dynamic_index_in_dim(halves, 1 - core, 0, keepdims=False)
    mine = sum_direct(mine + send(theirs, "core", 1), "x")
    other = send(mine, "core", 1)
    return jnp.where(core == 0, jnp.stack([mine, other]), jnp.stack([other, mine])).reshape(gram.shape)


def product_kernel(transpose, spans, low, plain, coded, with_gram, count_ref, to_ref, from_ref, tiles_ref, *rest):
    pieces, rest = rest[: len(spans)], rest[len(spans) :]
    outs, rest = rest[: 2 * len(plain) + len(coded) + with_gram], rest[2 * len(plain) + len(coded) + with_gram :]
    held, total, slots, places, arrived, left = rest
    copies = [
        pltpu.make_async_copy(piece, held.at[pl.ds(start, length)], arrived.at[i])
        for i, (piece, (start, length)) in enumerate(zip(pieces, spans))
    ]
    for copy in copies:
        copy.start()
    total[...] = jnp.zeros_like(total)
    blocks_here = sum(plain) + sum(coded)

    def choose(i, found):
        place = to_ref[i] - low
        slots[found] = i
        places[found] = place
        return found + jnp.where((place >= 0) & (place < blocks_here), 1, 0)

    found = lax.fori_loop(0, count_ref[0], choose, 0)
    for j in range(GROUP):
        slots[found + j] = 0
        places[found + j] = blocks_here
    for copy in copies:
        copy.wait()
    dims = (((0,), (0,)), ((), ())) if transpose else (((1,), (0,)), ((), ()))

    def step(i, carry):
        products = []
        for j in range(GROUP):
            slot = slots[i * GROUP + j]
            products.append(
                lax.dot_general(tiles_ref[slot], held[from_ref[slot]], dims, preferred_element_type=f32)
            )
        for j in range(GROUP):
            total[places[i * GROUP + j]] += products[j]
        return carry

    lax.fori_loop(0, (found + GROUP - 1) // GROUP, step, 0)
    start = 0
    copies = []
    for k, blocks in enumerate(plain):
        copies.append(pltpu.make_async_copy(total.at[pl.ds(start, blocks)], outs[2 * k], left.at[k]))
        copies[-1].start()
        start += blocks

    def bound_of(start, blocks):
        def widen(i, bound):
            return jnp.maximum(bound, jnp.max(jnp.abs(total[start + i]), axis=0, keepdims=True))

        return lax.fori_loop(0, blocks, widen, jnp.zeros((1, total.shape[2]), f32))

    start = 0
    for k, blocks in enumerate(plain):
        bound_ref = outs[2 * k + 1]
        if transpose:
            bound_ref[...] = bound_of(start, blocks)
        else:
            bound_ref[...] = jnp.zeros_like(bound_ref)
        start += blocks
    tile = total.shape[1]
    for k, blocks in enumerate(coded):
        out_ref = outs[2 * len(plain) + k]
        power, scale = power_of(bound_of(start, blocks))

        def finish(i, carry, out_ref=out_ref, start=start, scale=scale):
            rows = pl.ds(pl.multiple_of(i * tile, tile), tile)
            out_ref[rows, :] = jnp.round(total[start + i] * scale).astype(jnp.int32).astype(jnp.int16)
            return carry

        lax.fori_loop(0, blocks, finish, 0)
        out_ref[blocks * tile :, :] = jnp.broadcast_to(power, (TAIL, power.shape[1])).astype(jnp.int32).astype(jnp.int16)
        start += blocks
    if with_gram:
        gram_ref = outs[-1]
        gram_ref[...] = jnp.zeros_like(gram_ref)

        def add(i, carry):
            block = held[pl.ds(i * GROUP, GROUP)].reshape(GROUP * tile, -1)
            gram_ref[...] += lax.dot_general(block, block, (((0,), (0,)), ((), ())), preferred_element_type=f32)
            return carry

        lax.fori_loop(0, held.shape[0] // GROUP, add, 0)
    for copy in copies:
        copy.wait()


def product(tiles, pieces, to, source, count, low, plain, coded, transpose, with_gram=False):
    slots, tile, _ = tiles.shape
    width = pieces[0].shape[1]
    pieces = [piece.reshape(-1, tile, width) for piece in pieces]
    spans, start = [], 0
    for piece in pieces:
        spans.append((start, piece.shape[0]))
        start += piece.shape[0]
    outs = sum(plain) + sum(coded)
    smem = pl.BlockSpec(memory_space=pltpu.SMEM)
    vmem = pl.BlockSpec(memory_space=pltpu.VMEM)
    shapes = []
    for blocks in plain:
        shapes += [jax.ShapeDtypeStruct((blocks, tile, width), f32), jax.ShapeDtypeStruct((1, width), f32)]
    shapes += [jax.ShapeDtypeStruct((blocks * tile + TAIL, width), jnp.int16) for blocks in coded]
    shapes += [jax.ShapeDtypeStruct((width, width), f32)] * with_gram
    found = pl.pallas_call(
        functools.partial(product_kernel, transpose, tuple(spans), low, plain, coded, with_gram),
        out_shape=shapes,
        in_specs=[smem, smem, smem, vmem] + [pl.BlockSpec(memory_space=pl.ANY)] * len(pieces),
        out_specs=[pl.BlockSpec(memory_space=pl.ANY), vmem] * len(plain) + [vmem] * (len(coded) + with_gram),
        scratch_shapes=[
            pltpu.VMEM((start, tile, width), bf16),
            pltpu.VMEM((outs + 1, tile, width), f32),
            pltpu.SMEM((slots + GROUP,), jnp.int32),
            pltpu.SMEM((slots + GROUP,), jnp.int32),
            pltpu.SemaphoreType.DMA((len(pieces),)),
            pltpu.SemaphoreType.DMA((max(len(plain), 1),)),
        ],
        compiler_params=pltpu.CompilerParams(vmem_limit_bytes=48 * MIB),
        cost_estimate=pl.CostEstimate(
            flops=2 * slots * tile * tile * width,
            bytes_accessed=2 * (slots * tile * tile + (start + 2 * outs) * tile * width),
            transcendentals=0,
        ),
    )(count, to, source, tiles, *pieces)
    return [x.reshape(-1, width) for x in found]


def gram_of(panel):
    return lax.dot_general(panel, panel, (((0,), (0,)), ((), ())), precision=highest)


def apply_factor(panel, inverse):
    return lax.dot_general(panel, inverse, (((1,), (1,)), ((), ())), precision=highest)


def factor_kernel(gram_ref, out_ref, work):
    order = gram_ref.shape[0]
    shape = (BLOCK, 128)
    row_id = lax.broadcasted_iota(jnp.int32, shape, 0)
    unit = jnp.where(row_id == lax.broadcasted_iota(jnp.int32, shape, 1), 1.0, 0.0)
    work[:, :order] = gram_ref[...]
    square = (order, order)
    work[:, order:] = jnp.where(
        lax.broadcasted_iota(jnp.int32, square, 0) == lax.broadcasted_iota(jnp.int32, square, 1), 1.0, 0.0
    )
    for low in range(0, order, BLOCK):
        group = low // 128 * 128
        left = work[low : low + BLOCK, group : group + 128]
        right = unit
        pivots = jnp.ones(shape, f32)
        for start in range(0, BLOCK, PIVOTS):
            lane = low - group + start
            columns = [
                jnp.broadcast_to(left[:, lane + m : lane + m + 1], shape) for m in range(PIVOTS)
            ]
            for m in range(PIVOTS):
                at = start + m
                column = columns[m]
                pivot = jnp.broadcast_to(column[at : at + 1], shape)
                pivots = jnp.where(row_id == at, pivot, pivots)
                weight = jnp.where(row_id > at, column * (1.0 / pivot), 0.0)
                for q in range(m + 1, PIVOTS):
                    columns[q] = columns[q] - weight * column[start + q : start + q + 1]
                left = left - weight * left[at : at + 1]
                right = right - weight * right[at : at + 1]
        root = lax.rsqrt(pivots)
        root = root * (1.5 - 0.5 * pivots * root * root)
        right = right * root
        rows = jnp.dot(
            right[:, :BLOCK], work[low : low + BLOCK, :], precision=highest, preferred_element_type=f32
        )
        out_ref[low : low + BLOCK, :] = rows[:, order:]
        if low + BLOCK < order:
            update = lax.dot_general(
                rows[:, :order], rows, (((0,), (0,)), ((), ())), precision=highest, preferred_element_type=f32
            )
            work[low + BLOCK :, :] -= update[low + BLOCK :, :]


def inverse_factor(gram):
    order = gram.shape[0]
    return pl.pallas_call(
        factor_kernel,
        out_shape=jax.ShapeDtypeStruct(gram.shape, f32),
        scratch_shapes=[pltpu.VMEM((order, 2 * order), f32)],
        compiler_params=pltpu.CompilerParams(vmem_limit_bytes=16 * MIB),
        cost_estimate=pl.CostEstimate(flops=12 * GIGA, bytes_accessed=40 * MIB, transcendentals=0),
    )(gram)


def on_device(omega, tiles, coords):
    tile = tiles.shape[-1]
    factor = math.sqrt(omega.shape[0] * 256)
    local_tiles = tiles.reshape(tiles.shape[2], tile, tile)
    pairs = coords.reshape(coords.shape[2], 2)
    live = pairs[:, 0] >= 0
    count = jnp.sum(live.astype(jnp.int32)).reshape(1)
    my_y, my_z = lax.axis_index("y"), lax.axis_index("z")
    my_x, my_core = lax.axis_index("x"), lax.axis_index("core")

    local_row = jnp.clip(pairs[:, 0] - (my_y * 8 + my_z) * 16, 0, 15)
    keeper = local_row // 2
    row_slot = ((keeper + my_core) % 2 * 4 + (keeper // 2 - my_x + 4) % 4) * 2 + local_row % 2
    block_col = jnp.maximum(pairs[:, 1], 0)
    owner = block_col // 16
    far_y = (owner // 8 - my_y + 4) % 4
    far_z = (owner % 8 - my_z + 8) % 8
    panel_slot = jnp.where(block_col % 2 == 0, far_y * 8 + owner % 8, 32 + far_z * 4 + far_y)
    order_y = jnp.where(far_y == 2, 3, jnp.where(far_y == 3, 2, far_y))
    column_slot = (order_y * 8 + owner % 8) * 2 + block_col % 2
    row_to = jnp.where(live, row_slot, 16)
    column_to = jnp.where(live, column_slot, 64)

    def forward(panel, with_gram=False):
        pieces = gather_rows(panel.astype(bf16))
        return product(local_tiles, pieces, row_to, panel_slot, count, 0, (8, 8), (), False, with_gram)

    one = sum_cols(exchange_cols(forward(omega)))
    pieces = gather_cols(one.astype(bf16))
    far = product(local_tiles, pieces, column_to, row_slot, count, 48, (), (8, 8), True)
    *far, pieces[0] = together(*far, pieces[0])
    first, second = send(far[0], "y", 1), send(far[1], "y", -1)
    shares = product(local_tiles, pieces, column_to, row_slot, count, 0, (16, 16, 16), (), True)
    held_back, *shares = together(one, *shares)
    total, one_inverse = sum_rows(first, second, shares, gram_of(held_back))
    two = apply_factor(total, one_inverse)
    *shares, gram = forward(two, True)
    parts = exchange_cols(shares)
    gram, *parts = together(sum_over_cols(gram), *parts)
    two_inverse = inverse_factor(gram)
    three = apply_factor(sum_cols(parts), two_inverse)
    three_inverse = inverse_factor(gram_back(sum_along_z(sum_direct(gram_near(gram_of(three)), "y"))))
    return (
        apply_factor(three, three_inverse) * factor,
        apply_factor(one, one_inverse) * factor,
        apply_factor(two, two_inverse) * factor,
    )


def solution(mesh):
    mesh = Mesh(mesh.devices.reshape([SIZE[name] for name in AXES]), AXES)
    rows, cols = ("y", "z"), ("x", "core")
    return jax.shard_map(
        on_device,
        mesh=mesh,
        in_specs=(P(AXES, None), P(rows, cols, None, None, None), P(rows, cols, None, None)),
        out_specs=(P(AXES, None),) * 3,
        check_vma=False,
    )
```

```python
import functools
import math

import jax
import jax.numpy as jnp
from jax import lax
from jax.experimental import pallas as pl
from jax.experimental.pallas import tpu as pltpu
from jax.sharding import Mesh, PartitionSpec as P

highest = lax.Precision.HIGHEST
f32 = jnp.float32
bf16 = jnp.bfloat16
AXES = ("y", "z", "x", "core")
SIZE = {"y": 4, "z": 8, "x": 4, "core": 2}
GROUP = 4
BLOCK = 64
PIVOTS = 16
TAIL = 16
LEVELS = 16383.0
MIB = 1024 * 1024
GIGA = 1000**3


def send(value, axis, step):
    size = SIZE[axis]
    return lax.ppermute(value, axis, [(i, (i + step) % size) for i in range(size)])


def ring_gather(piece, axis):
    size = SIZE[axis]
    half = size // 2
    cut = piece.shape[0] // 2
    got = {0: piece}
    down = up = piece
    for k in range(1, half):
        down = send(down, axis, -1)
        up = send(up, axis, 1)
        got[k], got[size - k] = down, up
    first = send(down[:cut], axis, -1)
    second = send(up[cut:], axis, 1)
    return [got[k] for k in range(half)] + [first, second] + [got[k] for k in range(half + 1, size)]


def largest(value):
    return jnp.max(jnp.abs(value), axis=-2, keepdims=True)


def power_of(bound):
    power = jnp.clip(jnp.ceil(jnp.log2(jnp.maximum(bound, 1e-36))), -119, 119)
    return power, jnp.exp2(-power) * LEVELS


def encode(value, bound):
    power, scale = power_of(bound)
    whole = jnp.round(value * scale).astype(jnp.int16)
    tail = jnp.broadcast_to(power.astype(jnp.int16), value.shape[:-2] + (TAIL, value.shape[-1]))
    return jnp.concatenate([whole, tail], axis=-2)


def decode(message):
    bound = jnp.exp2(message[..., -1:, :].astype(f32))
    return message[..., :-TAIL, :].astype(f32) * (bound * (1 / LEVELS)), bound


def together(*values):
    return lax.optimization_barrier(values)


def direct_gather(piece, axis):
    size = SIZE[axis]
    return [piece] + [send(piece, axis, -k if k <= size // 2 else size - k) for k in range(1, size)]


def gather_rows(panel):
    tile = panel.shape[0] // 2
    two = jnp.concatenate(direct_gather(panel[tile:], "y"))
    one = jnp.broadcast_to(panel[:tile], (8, tile, panel.shape[1])).reshape(8 * tile, -1)
    one = lax.all_to_all(one, "z", split_axis=0, concat_axis=0, tiled=True)
    return ring_gather(one, "y") + ring_gather(two, "z")


def sum_rows(first, second, shares, gram):
    near, _, up, up_bound, down, down_bound = shares
    cut = near.shape[0] // 2
    first, first_bound = decode(first)
    second, second_bound = decode(second)
    up = jnp.concatenate([up[:cut] + first, up[cut:]])
    down = jnp.concatenate([down[:cut], down[cut:] + second])
    up = send(encode(up, up_bound + first_bound), "y", 1)
    down = send(encode(down, down_bound + second_bound), "y", -1)
    gram = sum_along_z(gram_over_x(gram))
    up, down, gram = together(up, down, gram)
    total = (near + decode(up)[0] + decode(down)[0]).reshape(8, -1, near.shape[1])
    messages = encode(total, largest(total))
    rows = messages.shape[1]
    messages = lax.all_to_all(messages.reshape(8 * rows, -1), "z", split_axis=0, concat_axis=0, tiled=True)
    inverse = inverse_factor(gram_back(sum_direct(gram, "y")))
    messages, inverse = together(messages, inverse)
    return jnp.sum(decode(messages.reshape(8, rows, -1))[0], axis=0), inverse


def gather_cols(panel):
    near = jnp.concatenate(ring_gather(panel, "x"))
    return [near, send(near, "core", 1)]


def exchange_cols(shares):
    near, _, far, _ = shares
    both = (near + send(far, "core", 1)).reshape(4, -1, near.shape[1])
    messages = encode(both, largest(both))
    return [both[0]] + [send(messages[k], "x", k if k < 3 else -1) for k in range(1, 4)]


def sum_cols(parts):
    return functools.reduce(jnp.add, [decode(message)[0] for message in parts[1:]], parts[0])


def sum_direct(value, axis):
    size = SIZE[axis]
    moved = [send(value, axis, k if k <= size // 2 else k - size) for k in range(1, size)]
    return functools.reduce(jnp.add, moved, value)


def sum_flipped(value, axis, flips):
    moved = [lax.ppermute(value, axis, [(i, i ^ flip) for i in range(SIZE[axis])]) for flip in flips]
    return functools.reduce(jnp.add, moved, value)


def sum_parts(gram, axes, count):
    parts = lax.all_to_all(gram, axes, split_axis=0, concat_axis=0, tiled=True)
    return jnp.sum(parts.reshape(count, -1, gram.shape[1]), axis=0)


def spread(part, axes, count):
    copies = jnp.broadcast_to(part, (count,) + part.shape).reshape(-1, part.shape[1])
    return lax.all_to_all(copies, axes, split_axis=0, concat_axis=0, tiled=True)


def sum_everywhere(gram):
    part = sum_parts(gram, ("y", "x", "core"), 32)
    part = jnp.sum(spread(part, "z", 8).reshape((8,) + part.shape), axis=0)
    return spread(part, ("y", "x", "core"), 32)


def gram_over_core(gram):
    core = lax.axis_index("core")
    quads = gram.reshape(2, 4, -1, gram.shape[1])
    mine = lax.dynamic_index_in_dim(quads, core, 0, keepdims=False)
    theirs = lax.dynamic_index_in_dim(quads, 1 - core, 0, keepdims=False)
    return mine + send(theirs, "core", 1)


def gram_over_x(mine):
    place = lax.axis_index("x")

    def pick(k):
        return lax.dynamic_index_in_dim(mine, lax.rem(place + k, 4), 0, keepdims=False)

    return pick(0) + send(pick(1), "x", 1) + send(pick(2), "x", 2) + send(pick(3), "x", -1)


def sum_along_z(part):
    return sum_flipped(sum_flipped(part, "z", (1, 2, 3)), "z", (4,))


def gram_back(part):
    core = lax.axis_index("core")
    place = lax.axis_index("x")
    got = jnp.stack([part, send(part, "x", -1), send(part, "x", 2), send(part, "x", 1)])
    back = jnp.stack(
        [lax.dynamic_index_in_dim(got, lax.rem(k - place + 4, 4), 0, keepdims=False) for k in range(4)]
    )
    other = send(back, "core", 1)
    both = jnp.where(core == 0, jnp.stack([back, other]), jnp.stack([other, back]))
    return both.reshape(-1, part.shape[1])


def sum_over_cols(gram):
    core = lax.axis_index("core")
    halves = gram.reshape(2, -1, gram.shape[1])
    mine = lax.dynamic_index_in_dim(halves, core, 0, keepdims=False)
    theirs = lax.dynamic_index_in_dim(halves, 1 - core, 0, keepdims=False)
    mine = sum_direct(mine + send(theirs, "core", 1), "x")
    other = send(mine, "core", 1)
    return jnp.where(core == 0, jnp.stack([mine, other]), jnp.stack([other, mine])).reshape(gram.shape)


def product_kernel(transpose, spans, low, plain, coded, with_gram, count_ref, to_ref, from_ref, tiles_ref, *rest):
    pieces, rest = rest[: len(spans)], rest[len(spans) :]
    outs, rest = rest[: 2 * len(plain) + len(coded) + with_gram], rest[2 * len(plain) + len(coded) + with_gram :]
    held, total, slots, places, arrived, left = rest
    copies = [
        pltpu.make_async_copy(piece, held.at[pl.ds(start, length)], arrived.at[i])
        for i, (piece, (start, length)) in enumerate(zip(pieces, spans))
    ]
    for copy in copies:
        copy.start()
    total[...] = jnp.zeros_like(total)
    blocks_here = sum(plain) + sum(coded)

    def choose(i, found):
        place = to_ref[i] - low
        slots[found] = i
        places[found] = place
        return found + jnp.where((place >= 0) & (place < blocks_here), 1, 0)

    found = lax.fori_loop(0, count_ref[0], choose, 0)
    for j in range(GROUP):
        slots[found + j] = 0
        places[found + j] = blocks_here
    for copy in copies:
        copy.wait()
    dims = (((0,), (0,)), ((), ())) if transpose else (((1,), (0,)), ((), ()))

    def step(i, carry):
        products = []
        for j in range(GROUP):
            slot = slots[i * GROUP + j]
            products.append(
                lax.dot_general(tiles_ref[slot], held[from_ref[slot]], dims, preferred_element_type=f32)
            )
        for j in range(GROUP):
            total[places[i * GROUP + j]] += products[j]
        return carry

    lax.fori_loop(0, (found + GROUP - 1) // GROUP, step, 0)
    start = 0
    copies = []
    for k, blocks in enumerate(plain):
        copies.append(pltpu.make_async_copy(total.at[pl.ds(start, blocks)], outs[2 * k], left.at[k]))
        copies[-1].start()
        start += blocks

    def bound_of(start, blocks):
        def widen(i, bound):
            return jnp.maximum(bound, jnp.max(jnp.abs(total[start + i]), axis=0, keepdims=True))

        return lax.fori_loop(0, blocks, widen, jnp.zeros((1, total.shape[2]), f32))

    start = 0
    for k, blocks in enumerate(plain):
        bound_ref = outs[2 * k + 1]
        if transpose:
            bound_ref[...] = bound_of(start, blocks)
        else:
            bound_ref[...] = jnp.zeros_like(bound_ref)
        start += blocks
    tile = total.shape[1]
    for k, blocks in enumerate(coded):
        out_ref = outs[2 * len(plain) + k]
        power, scale = power_of(bound_of(start, blocks))

        def finish(i, carry, out_ref=out_ref, start=start, scale=scale):
            rows = pl.ds(pl.multiple_of(i * tile, tile), tile)
            out_ref[rows, :] = jnp.round(total[start + i] * scale).astype(jnp.int32).astype(jnp.int16)
            return carry

        lax.fori_loop(0, blocks, finish, 0)
        out_ref[blocks * tile :, :] = jnp.broadcast_to(power, (TAIL, power.shape[1])).astype(jnp.int32).astype(jnp.int16)
        start += blocks
    if with_gram:
        gram_ref = outs[-1]
        gram_ref[...] = jnp.zeros_like(gram_ref)

        def add(i, carry):
            block = held[pl.ds(i * GROUP, GROUP)].reshape(GROUP * tile, -1)
            gram_ref[...] += lax.dot_general(block, block, (((0,), (0,)), ((), ())), preferred_element_type=f32)
            return carry

        lax.fori_loop(0, held.shape[0] // GROUP, add, 0)
    for copy in copies:
        copy.wait()


def product(tiles, pieces, to, source, count, low, plain, coded, transpose, with_gram=False):
    slots, tile, _ = tiles.shape
    width = pieces[0].shape[1]
    pieces = [piece.reshape(-1, tile, width) for piece in pieces]
    spans, start = [], 0
    for piece in pieces:
        spans.append((start, piece.shape[0]))
        start += piece.shape[0]
    outs = sum(plain) + sum(coded)
    smem = pl.BlockSpec(memory_space=pltpu.SMEM)
    vmem = pl.BlockSpec(memory_space=pltpu.VMEM)
    shapes = []
    for blocks in plain:
        shapes += [jax.ShapeDtypeStruct((blocks, tile, width), f32), jax.ShapeDtypeStruct((1, width), f32)]
    shapes += [jax.ShapeDtypeStruct((blocks * tile + TAIL, width), jnp.int16) for blocks in coded]
    shapes += [jax.ShapeDtypeStruct((width, width), f32)] * with_gram
    found = pl.pallas_call(
        functools.partial(product_kernel, transpose, tuple(spans), low, plain, coded, with_gram),
        out_shape=shapes,
        in_specs=[smem, smem, smem, vmem] + [pl.BlockSpec(memory_space=pl.ANY)] * len(pieces),
        out_specs=[pl.BlockSpec(memory_space=pl.ANY), vmem] * len(plain) + [vmem] * (len(coded) + with_gram),
        scratch_shapes=[
            pltpu.VMEM((start, tile, width), bf16),
            pltpu.VMEM((outs + 1, tile, width), f32),
            pltpu.SMEM((slots + GROUP,), jnp.int32),
            pltpu.SMEM((slots + GROUP,), jnp.int32),
            pltpu.SemaphoreType.DMA((len(pieces),)),
            pltpu.SemaphoreType.DMA((max(len(plain), 1),)),
        ],
        compiler_params=pltpu.CompilerParams(vmem_limit_bytes=48 * MIB),
        cost_estimate=pl.CostEstimate(
            flops=2 * slots * tile * tile * width,
            bytes_accessed=2 * (slots * tile * tile + (start + 2 * outs) * tile * width),
            transcendentals=0,
        ),
    )(count, to, source, tiles, *pieces)
    return [x.reshape(-1, width) for x in found]


def gram_of(panel):
    return lax.dot_general(panel, panel, (((0,), (0,)), ((), ())), precision=highest)


def apply_factor(panel, inverse):
    return lax.dot_general(panel, inverse, (((1,), (1,)), ((), ())), precision=highest)


def factor_kernel(gram_ref, out_ref, work):
    order = gram_ref.shape[0]
    shape = (BLOCK, 128)
    row_id = lax.broadcasted_iota(jnp.int32, shape, 0)
    unit = jnp.where(row_id == lax.broadcasted_iota(jnp.int32, shape, 1), 1.0, 0.0)
    work[:, :order] = gram_ref[...]
    square = (order, order)
    work[:, order:] = jnp.where(
        lax.broadcasted_iota(jnp.int32, square, 0) == lax.broadcasted_iota(jnp.int32, square, 1), 1.0, 0.0
    )
    for low in range(0, order, BLOCK):
        group = low // 128 * 128
        left = work[low : low + BLOCK, group : group + 128]
        right = unit
        pivots = jnp.ones(shape, f32)
        for start in range(0, BLOCK, PIVOTS):
            lane = low - group + start
            columns = [
                jnp.broadcast_to(left[:, lane + m : lane + m + 1], shape) for m in range(PIVOTS)
            ]
            for m in range(PIVOTS):
                at = start + m
                column = columns[m]
                pivot = jnp.broadcast_to(column[at : at + 1], shape)
                pivots = jnp.where(row_id == at, pivot, pivots)
                weight = jnp.where(row_id > at, column * (1.0 / pivot), 0.0)
                for q in range(m + 1, PIVOTS):
                    columns[q] = columns[q] - weight * column[start + q : start + q + 1]
                left = left - weight * left[at : at + 1]
                right = right - weight * right[at : at + 1]
        root = lax.rsqrt(pivots)
        root = root * (1.5 - 0.5 * pivots * root * root)
        right = right * root
        rows = jnp.dot(
            right[:, :BLOCK], work[low : low + BLOCK, :], precision=highest, preferred_element_type=f32
        )
        out_ref[low : low + BLOCK, :] = rows[:, order:]
        if low + BLOCK < order:
            update = lax.dot_general(
                rows[:, :order], rows, (((0,), (0,)), ((), ())), precision=highest, preferred_element_type=f32
            )
            work[low + BLOCK :, :] -= update[low + BLOCK :, :]


def inverse_factor(gram):
    order = gram.shape[0]
    return pl.pallas_call(
        factor_kernel,
        out_shape=jax.ShapeDtypeStruct(gram.shape, f32),
        scratch_shapes=[pltpu.VMEM((order, 2 * order), f32)],
        compiler_params=pltpu.CompilerParams(vmem_limit_bytes=16 * MIB),
        cost_estimate=pl.CostEstimate(flops=12 * GIGA, bytes_accessed=40 * MIB, transcendentals=0),
    )(gram)


def on_device(omega, tiles, coords):
    tile = tiles.shape[-1]
    factor = math.sqrt(omega.shape[0] * 256)
    local_tiles = tiles.reshape(tiles.shape[2], tile, tile)
    pairs = coords.reshape(coords.shape[2], 2)
    live = pairs[:, 0] >= 0
    count = jnp.sum(live.astype(jnp.int32)).reshape(1)
    my_y, my_z = lax.axis_index("y"), lax.axis_index("z")
    my_x, my_core = lax.axis_index("x"), lax.axis_index("core")

    local_row = jnp.clip(pairs[:, 0] - (my_y * 8 + my_z) * 16, 0, 15)
    keeper = local_row // 2
    row_slot = ((keeper + my_core) % 2 * 4 + (keeper // 2 - my_x + 4) % 4) * 2 + local_row % 2
    block_col = jnp.maximum(pairs[:, 1], 0)
    owner = block_col // 16
    far_y = (owner // 8 - my_y + 4) % 4
    far_z = (owner % 8 - my_z + 8) % 8
    panel_slot = jnp.where(block_col % 2 == 0, far_y * 8 + owner % 8, 32 + far_z * 4 + far_y)
    order_y = jnp.where(far_y == 2, 3, jnp.where(far_y == 3, 2, far_y))
    column_slot = (order_y * 8 + owner % 8) * 2 + block_col % 2
    row_to = jnp.where(live, row_slot, 16)
    column_to = jnp.where(live, column_slot, 64)

    def forward(panel, with_gram=False):
        pieces = gather_rows(panel.astype(bf16))
        return product(local_tiles, pieces, row_to, panel_slot, count, 0, (8, 8), (), False, with_gram)

    one = sum_cols(exchange_cols(forward(omega)))
    pieces = gather_cols(one.astype(bf16))
    far = product(local_tiles, pieces, column_to, row_slot, count, 48, (), (8, 8), True)
    *far, pieces[0], held_back = together(*far, pieces[0], one)
    first, second = send(far[0], "y", 1), send(far[1], "y", -1)
    shares = product(local_tiles, pieces, column_to, row_slot, count, 0, (16, 16, 16), (), True)
    gram = gram_over_core(gram_of(held_back))
    first, second, gram, *shares = together(first, second, gram, *shares)
    total, one_inverse = sum_rows(first, second, shares, gram)
    two = apply_factor(total, one_inverse)
    *shares, gram = forward(two, True)
    parts = exchange_cols(shares)
    gram, *parts = together(sum_over_cols(gram), *parts)
    two_inverse = inverse_factor(gram)
    three = apply_factor(sum_cols(parts), two_inverse)
    three_inverse = inverse_factor(sum_everywhere(gram_of(three)))
    return (
        apply_factor(three, three_inverse) * factor,
        apply_factor(one, one_inverse) * factor,
        apply_factor(two, two_inverse) * factor,
    )


def solution(mesh):
    mesh = Mesh(mesh.devices.reshape([SIZE[name] for name in AXES]), AXES)
    rows, cols = ("y", "z"), ("x", "core")
    return jax.shard_map(
        on_device,
        mesh=mesh,
        in_specs=(P(AXES, None), P(rows, cols, None, None, None), P(rows, cols, None, None)),
        out_specs=(P(AXES, None),) * 3,
        check_vma=False,
    )
```

```python
import functools
import math

import jax
import jax.numpy as jnp
from jax import lax
from jax.experimental import pallas as pl
from jax.experimental.pallas import tpu as pltpu
from jax.sharding import Mesh, PartitionSpec as P

highest = lax.Precision.HIGHEST
f32 = jnp.float32
bf16 = jnp.bfloat16
AXES = ("y", "z", "x", "core")
SIZE = {"y": 4, "z": 8, "x": 4, "core": 2}
GROUP = 4
BLOCK = 64
PIVOTS = 16
TAIL = 16
LEVELS = 16383.0
CHUNK = 128
MIB = 1024 * 1024
GIGA = 1000**3


def send(value, axis, step):
    size = SIZE[axis]
    return lax.ppermute(value, axis, [(i, (i + step) % size) for i in range(size)])


def ring_gather(piece, axis):
    size = SIZE[axis]
    half = size // 2
    cut = piece.shape[0] // 2
    got = {0: piece}
    down = up = piece
    for k in range(1, half):
        down = send(down, axis, -1)
        up = send(up, axis, 1)
        got[k], got[size - k] = down, up
    first = send(down[:cut], axis, -1)
    second = send(up[cut:], axis, 1)
    return [got[k] for k in range(half)] + [first, second] + [got[k] for k in range(half + 1, size)]


def largest(value):
    return jnp.max(jnp.abs(value), axis=-2, keepdims=True)


def power_of(bound):
    power = jnp.clip(jnp.ceil(jnp.log2(jnp.maximum(bound, 1e-36))), -119, 119)
    return power, jnp.exp2(-power) * LEVELS


def encode(value, bound):
    power, scale = power_of(bound)
    whole = jnp.round(value * scale).astype(jnp.int16)
    tail = jnp.broadcast_to(power.astype(jnp.int16), value.shape[:-2] + (TAIL, value.shape[-1]))
    return jnp.concatenate([whole, tail], axis=-2)


def decode(message):
    bound = jnp.exp2(message[..., -1:, :].astype(f32))
    return message[..., :-TAIL, :].astype(f32) * (bound * (1 / LEVELS)), bound


def together(*values):
    return lax.optimization_barrier(values)


def whole(value):
    return jnp.round(value).astype(jnp.int32).astype(jnp.int16)


def relay_kernel(first, part_ref, bound_ref, message_ref, out_ref):
    rows = part_ref.shape[0]
    arrived = message_ref.shape[0] - TAIL
    bound = jnp.exp2(message_ref[arrived:, :].astype(jnp.int32).astype(f32)[:1])
    power, scale = power_of(bound_ref[...] + bound)
    step = bound * (1 / LEVELS)

    def add(i, carry):
        here = pl.ds(pl.multiple_of(i * CHUNK, CHUNK), CHUNK)
        there = pl.ds(pl.multiple_of(first + i * CHUNK, CHUNK), CHUNK)
        value = part_ref[there, :] + message_ref[here, :].astype(jnp.int32).astype(f32) * step
        out_ref[there, :] = whole(value * scale)
        return carry

    def keep(i, carry):
        there = pl.ds(pl.multiple_of(arrived - first + i * CHUNK, CHUNK), CHUNK)
        out_ref[there, :] = whole(part_ref[there, :] * scale)
        return carry

    lax.fori_loop(0, arrived // CHUNK, add, 0)
    lax.fori_loop(0, (rows - arrived) // CHUNK, keep, 0)
    out_ref[rows:, :] = jnp.broadcast_to(power, (TAIL, power.shape[1])).astype(jnp.int32).astype(jnp.int16)


def relay(first, part, bound, message):
    return pl.pallas_call(
        functools.partial(relay_kernel, first),
        out_shape=jax.ShapeDtypeStruct((part.shape[0] + TAIL, part.shape[1]), jnp.int16),
        compiler_params=pltpu.CompilerParams(vmem_limit_bytes=24 * MIB),
        cost_estimate=pl.CostEstimate(flops=0, bytes_accessed=8 * part.size, transcendentals=0),
    )(part, bound, message)


def settle_kernel(near_ref, up_ref, down_ref, out_ref, total):
    count, rows = out_ref.shape[0], out_ref.shape[1] - TAIL
    size = near_ref.shape[0]
    up_step = jnp.exp2(up_ref[size:, :].astype(jnp.int32).astype(f32)[:1]) * (1 / LEVELS)
    down_step = jnp.exp2(down_ref[size:, :].astype(jnp.int32).astype(f32)[:1]) * (1 / LEVELS)

    def group(k, carry):
        bound = jnp.zeros(up_step.shape, f32)
        for start in range(0, rows, CHUNK):
            here = pl.ds(pl.multiple_of(k * rows + start, CHUNK), CHUNK)
            value = near_ref[here, :] + up_ref[here, :].astype(jnp.int32).astype(f32) * up_step
            value = value + down_ref[here, :].astype(jnp.int32).astype(f32) * down_step
            total[start : start + CHUNK, :] = value
            bound = jnp.maximum(bound, jnp.max(jnp.abs(value), axis=0, keepdims=True))
        power, scale = power_of(bound)
        out_ref[k, :rows, :] = whole(total[...] * scale)
        out_ref[k, rows:, :] = jnp.broadcast_to(power, (TAIL, power.shape[1])).astype(jnp.int32).astype(jnp.int16)
        return carry

    lax.fori_loop(0, count, group, 0)


def settle(near, up, down, count):
    rows, width = near.shape[0] // count, near.shape[1]
    return pl.pallas_call(
        settle_kernel,
        out_shape=jax.ShapeDtypeStruct((count, rows + TAIL, width), jnp.int16),
        scratch_shapes=[pltpu.VMEM((rows, width), f32)],
        compiler_params=pltpu.CompilerParams(vmem_limit_bytes=24 * MIB),
        cost_estimate=pl.CostEstimate(flops=0, bytes_accessed=10 * near.size, transcendentals=0),
    )(near, up, down)


def direct_gather(piece, axis):
    size = SIZE[axis]
    return [piece] + [send(piece, axis, -k if k <= size // 2 else size - k) for k in range(1, size)]


def gather_rows(panel):
    tile = panel.shape[0] // 2
    two = jnp.concatenate(direct_gather(panel[tile:], "y"))
    one = jnp.broadcast_to(panel[:tile], (8, tile, panel.shape[1])).reshape(8 * tile, -1)
    one = lax.all_to_all(one, "z", split_axis=0, concat_axis=0, tiled=True)
    return ring_gather(one, "y") + ring_gather(two, "z")


def sum_rows(first, second, shares, gram):
    near, _, up, up_bound, down, down_bound = shares
    cut = near.shape[0] // 2
    up = send(relay(0, up, up_bound, first), "y", 1)
    down = send(relay(cut, down, down_bound, second), "y", -1)
    gram = sum_along_z(gram_over_x(gram))
    up, down, gram = together(up, down, gram)
    messages = settle(near, up, down, 8)
    rows = messages.shape[1]
    messages = lax.all_to_all(messages.reshape(8 * rows, -1), "z", split_axis=0, concat_axis=0, tiled=True)
    inverse = inverse_factor(gram_back(sum_direct(gram, "y")))
    messages, inverse = together(messages, inverse)
    return jnp.sum(decode(messages.reshape(8, rows, -1))[0], axis=0), inverse


def gather_cols(panel):
    near = jnp.concatenate(ring_gather(panel, "x"))
    return [near, send(near, "core", 1)]


def exchange_cols(shares):
    near, _, far, _ = shares
    both = (near + send(far, "core", 1)).reshape(4, -1, near.shape[1])
    messages = encode(both, largest(both))
    return [both[0]] + [send(messages[k], "x", k if k < 3 else -1) for k in range(1, 4)]


def sum_cols(parts):
    return functools.reduce(jnp.add, [decode(message)[0] for message in parts[1:]], parts[0])


def sum_direct(value, axis):
    size = SIZE[axis]
    moved = [send(value, axis, k if k <= size // 2 else k - size) for k in range(1, size)]
    return functools.reduce(jnp.add, moved, value)


def sum_flipped(value, axis, flips):
    moved = [lax.ppermute(value, axis, [(i, i ^ flip) for i in range(SIZE[axis])]) for flip in flips]
    return functools.reduce(jnp.add, moved, value)


def sum_parts(gram, axes, count):
    parts = lax.all_to_all(gram, axes, split_axis=0, concat_axis=0, tiled=True)
    return jnp.sum(parts.reshape(count, -1, gram.shape[1]), axis=0)


def spread(part, axes, count):
    copies = jnp.broadcast_to(part, (count,) + part.shape).reshape(-1, part.shape[1])
    return lax.all_to_all(copies, axes, split_axis=0, concat_axis=0, tiled=True)


def sum_everywhere(gram):
    part = sum_parts(gram, ("y", "x", "core"), 32)
    part = jnp.sum(spread(part, "z", 8).reshape((8,) + part.shape), axis=0)
    return spread(part, ("y", "x", "core"), 32)


def gram_over_core(gram):
    core = lax.axis_index("core")
    quads = gram.reshape(2, 4, -1, gram.shape[1])
    mine = lax.dynamic_index_in_dim(quads, core, 0, keepdims=False)
    theirs = lax.dynamic_index_in_dim(quads, 1 - core, 0, keepdims=False)
    return mine + send(theirs, "core", 1)


def gram_over_x(mine):
    place = lax.axis_index("x")

    def pick(k):
        return lax.dynamic_index_in_dim(mine, lax.rem(place + k, 4), 0, keepdims=False)

    return pick(0) + send(pick(1), "x", 1) + send(pick(2), "x", 2) + send(pick(3), "x", -1)


def sum_along_z(part):
    return sum_flipped(sum_flipped(part, "z", (1, 2, 3)), "z", (4,))


def gram_back(part):
    core = lax.axis_index("core")
    place = lax.axis_index("x")
    got = jnp.stack([part, send(part, "x", -1), send(part, "x", 2), send(part, "x", 1)])
    back = jnp.stack(
        [lax.dynamic_index_in_dim(got, lax.rem(k - place + 4, 4), 0, keepdims=False) for k in range(4)]
    )
    other = send(back, "core", 1)
    both = jnp.where(core == 0, jnp.stack([back, other]), jnp.stack([other, back]))
    return both.reshape(-1, part.shape[1])


def sum_over_cols(gram):
    core = lax.axis_index("core")
    halves = gram.reshape(2, -1, gram.shape[1])
    mine = lax.dynamic_index_in_dim(halves, core, 0, keepdims=False)
    theirs = lax.dynamic_index_in_dim(halves, 1 - core, 0, keepdims=False)
    mine = sum_direct(mine + send(theirs, "core", 1), "x")
    other = send(mine, "core", 1)
    return jnp.where(core == 0, jnp.stack([mine, other]), jnp.stack([other, mine])).reshape(gram.shape)


def product_kernel(transpose, spans, low, plain, coded, with_gram, count_ref, to_ref, from_ref, tiles, *rest):
    pieces, rest = rest[: len(spans)], rest[len(spans) :]
    outs, rest = rest[: 2 * len(plain) + len(coded) + with_gram], rest[2 * len(plain) + len(coded) + with_gram :]
    held, tiles_ref, total, slots, places, arrived, left = rest
    copies = [
        pltpu.make_async_copy(piece, held.at[pl.ds(start, length)], arrived.at[i])
        for i, (piece, (start, length)) in enumerate(zip(pieces, spans))
    ]
    copies.append(pltpu.make_async_copy(tiles, tiles_ref, arrived.at[len(pieces)]))
    for copy in copies:
        copy.start()
    total[...] = jnp.zeros_like(total)
    blocks_here = sum(plain) + sum(coded)

    def choose(i, found):
        place = to_ref[i] - low
        slots[found] = i
        places[found] = place
        return found + jnp.where((place >= 0) & (place < blocks_here), 1, 0)

    found = lax.fori_loop(0, count_ref[0], choose, 0)
    for j in range(GROUP):
        slots[found + j] = 0
        places[found + j] = blocks_here
    for copy in copies:
        copy.wait()
    dims = (((0,), (0,)), ((), ())) if transpose else (((1,), (0,)), ((), ()))

    def step(i, carry):
        products = []
        for j in range(GROUP):
            slot = slots[i * GROUP + j]
            products.append(
                lax.dot_general(tiles_ref[slot], held[from_ref[slot]], dims, preferred_element_type=f32)
            )
        for j in range(GROUP):
            total[places[i * GROUP + j]] += products[j]
        return carry

    lax.fori_loop(0, (found + GROUP - 1) // GROUP, step, 0)
    start = 0
    copies = []
    for k, blocks in enumerate(plain):
        copies.append(pltpu.make_async_copy(total.at[pl.ds(start, blocks)], outs[2 * k], left.at[k]))
        copies[-1].start()
        start += blocks

    def bound_of(start, blocks):
        def widen(i, bound):
            return jnp.maximum(bound, jnp.max(jnp.abs(total[start + i]), axis=0, keepdims=True))

        return lax.fori_loop(0, blocks, widen, jnp.zeros((1, total.shape[2]), f32))

    start = 0
    for k, blocks in enumerate(plain):
        bound_ref = outs[2 * k + 1]
        if transpose and k:
            bound_ref[...] = bound_of(start, blocks)
        else:
            bound_ref[...] = jnp.zeros_like(bound_ref)
        start += blocks
    tile = total.shape[1]
    for k, blocks in enumerate(coded):
        out_ref = outs[2 * len(plain) + k]
        power, scale = power_of(bound_of(start, blocks))

        def finish(i, carry, out_ref=out_ref, start=start, scale=scale):
            rows = pl.ds(pl.multiple_of(i * tile, tile), tile)
            out_ref[rows, :] = whole(total[start + i] * scale)
            return carry

        lax.fori_loop(0, blocks, finish, 0)
        out_ref[blocks * tile :, :] = jnp.broadcast_to(power, (TAIL, power.shape[1])).astype(jnp.int32).astype(jnp.int16)
        start += blocks
    if with_gram:
        gram_ref = outs[-1]
        gram_ref[...] = jnp.zeros_like(gram_ref)

        def add(i, carry):
            block = held[pl.ds(i * GROUP, GROUP)].reshape(GROUP * tile, -1)
            gram_ref[...] += lax.dot_general(block, block, (((0,), (0,)), ((), ())), preferred_element_type=f32)
            return carry

        lax.fori_loop(0, held.shape[0] // GROUP, add, 0)
    for copy in copies:
        copy.wait()


def product(tiles, pieces, to, source, count, low, plain, coded, transpose, with_gram=False):
    slots, tile, _ = tiles.shape
    width = pieces[0].shape[1]
    pieces = [piece.reshape(-1, tile, width) for piece in pieces]
    spans, start = [], 0
    for piece in pieces:
        spans.append((start, piece.shape[0]))
        start += piece.shape[0]
    outs = sum(plain) + sum(coded)
    smem = pl.BlockSpec(memory_space=pltpu.SMEM)
    vmem = pl.BlockSpec(memory_space=pltpu.VMEM)
    shapes = []
    for blocks in plain:
        shapes += [jax.ShapeDtypeStruct((blocks, tile, width), f32), jax.ShapeDtypeStruct((1, width), f32)]
    shapes += [jax.ShapeDtypeStruct((blocks * tile + TAIL, width), jnp.int16) for blocks in coded]
    shapes += [jax.ShapeDtypeStruct((width, width), f32)] * with_gram
    found = pl.pallas_call(
        functools.partial(product_kernel, transpose, tuple(spans), low, plain, coded, with_gram),
        out_shape=shapes,
        in_specs=[smem, smem, smem] + [pl.BlockSpec(memory_space=pl.ANY)] * (1 + len(pieces)),
        out_specs=[pl.BlockSpec(memory_space=pl.ANY), vmem] * len(plain) + [vmem] * (len(coded) + with_gram),
        scratch_shapes=[
            pltpu.VMEM((start, tile, width), bf16),
            pltpu.VMEM((slots, tile, tile), bf16),
            pltpu.VMEM((outs + 1, tile, width), f32),
            pltpu.SMEM((slots + GROUP,), jnp.int32),
            pltpu.SMEM((slots + GROUP,), jnp.int32),
            pltpu.SemaphoreType.DMA((len(pieces) + 1,)),
            pltpu.SemaphoreType.DMA((max(len(plain), 1),)),
        ],
        compiler_params=pltpu.CompilerParams(vmem_limit_bytes=48 * MIB),
        cost_estimate=pl.CostEstimate(
            flops=2 * slots * tile * tile * width,
            bytes_accessed=2 * (slots * tile * tile + (start + 2 * outs) * tile * width),
            transcendentals=0,
        ),
    )(count, to, source, tiles, *pieces)
    return [x.reshape(-1, width) for x in found]


def gram_of(panel):
    return lax.dot_general(panel, panel, (((0,), (0,)), ((), ())), precision=highest)


def apply_factor(panel, inverse):
    return lax.dot_general(panel, inverse, (((1,), (1,)), ((), ())), precision=highest)


def factor_kernel(gram_ref, out_ref, work):
    order = gram_ref.shape[0]
    shape = (BLOCK, 128)
    row_id = lax.broadcasted_iota(jnp.int32, shape, 0)
    unit = jnp.where(row_id == lax.broadcasted_iota(jnp.int32, shape, 1), 1.0, 0.0)
    work[:, :order] = gram_ref[...]
    square = (order, order)
    work[:, order:] = jnp.where(
        lax.broadcasted_iota(jnp.int32, square, 0) == lax.broadcasted_iota(jnp.int32, square, 1), 1.0, 0.0
    )
    for low in range(0, order, BLOCK):
        group = low // 128 * 128
        left = work[low : low + BLOCK, group : group + 128]
        right = unit
        pivots = jnp.ones(shape, f32)
        for start in range(0, BLOCK, PIVOTS):
            lane = low - group + start
            columns = [
                jnp.broadcast_to(left[:, lane + m : lane + m + 1], shape) for m in range(PIVOTS)
            ]
            for m in range(PIVOTS):
                at = start + m
                column = columns[m]
                pivot = jnp.broadcast_to(column[at : at + 1], shape)
                pivots = jnp.where(row_id == at, pivot, pivots)
                weight = jnp.where(row_id > at, column * (1.0 / pivot), 0.0)
                for q in range(m + 1, PIVOTS):
                    columns[q] = columns[q] - weight * column[start + q : start + q + 1]
                left = left - weight * left[at : at + 1]
                right = right - weight * right[at : at + 1]
        root = lax.rsqrt(pivots)
        root = root * (1.5 - 0.5 * pivots * root * root)
        right = right * root
        rows = jnp.dot(
            right[:, :BLOCK], work[low : low + BLOCK, :], precision=highest, preferred_element_type=f32
        )
        out_ref[low : low + BLOCK, :] = rows[:, order:]
        if low + BLOCK < order:
            update = lax.dot_general(
                rows[:, :order], rows, (((0,), (0,)), ((), ())), precision=highest, preferred_element_type=f32
            )
            work[low + BLOCK :, :] -= update[low + BLOCK :, :]


def inverse_factor(gram):
    order = gram.shape[0]
    return pl.pallas_call(
        factor_kernel,
        out_shape=jax.ShapeDtypeStruct(gram.shape, f32),
        scratch_shapes=[pltpu.VMEM((order, 2 * order), f32)],
        compiler_params=pltpu.CompilerParams(vmem_limit_bytes=16 * MIB),
        cost_estimate=pl.CostEstimate(flops=12 * GIGA, bytes_accessed=40 * MIB, transcendentals=0),
    )(gram)


def on_device(omega, tiles, coords):
    tile = tiles.shape[-1]
    factor = math.sqrt(omega.shape[0] * 256)
    local_tiles = tiles.reshape(tiles.shape[2], tile, tile)
    pairs = coords.reshape(coords.shape[2], 2)
    live = pairs[:, 0] >= 0
    count = jnp.sum(live.astype(jnp.int32)).reshape(1)
    my_y, my_z = lax.axis_index("y"), lax.axis_index("z")
    my_x, my_core = lax.axis_index("x"), lax.axis_index("core")

    local_row = jnp.clip(pairs[:, 0] - (my_y * 8 + my_z) * 16, 0, 15)
    keeper = local_row // 2
    row_slot = ((keeper + my_core) % 2 * 4 + (keeper // 2 - my_x + 4) % 4) * 2 + local_row % 2
    block_col = jnp.maximum(pairs[:, 1], 0)
    owner = block_col // 16
    far_y = (owner // 8 - my_y + 4) % 4
    far_z = (owner % 8 - my_z + 8) % 8
    panel_slot = jnp.where(block_col % 2 == 0, far_y * 8 + owner % 8, 32 + far_z * 4 + far_y)
    order_y = jnp.where(far_y == 2, 3, jnp.where(far_y == 3, 2, far_y))
    column_slot = (order_y * 8 + owner % 8) * 2 + block_col % 2
    row_to = jnp.where(live, row_slot, 16)
    column_to = jnp.where(live, column_slot, 64)

    def forward(panel, with_gram=False):
        pieces = gather_rows(panel.astype(bf16))
        return product(local_tiles, pieces, row_to, panel_slot, count, 0, (8, 8), (), False, with_gram)

    one = sum_cols(exchange_cols(forward(omega)))
    pieces = gather_cols(one.astype(bf16))
    far = product(local_tiles, pieces, column_to, row_slot, count, 48, (), (8, 8), True)
    *far, pieces[0], held_back = together(*far, pieces[0], one)
    first, second = send(far[0], "y", 1), send(far[1], "y", -1)
    shares = product(local_tiles, pieces, column_to, row_slot, count, 0, (16, 16, 16), (), True)
    gram = gram_over_core(gram_of(held_back))
    first, second, gram, *shares = together(first, second, gram, *shares)
    total, one_inverse = sum_rows(first, second, shares, gram)
    two = apply_factor(total, one_inverse)
    *shares, gram = forward(two, True)
    parts = exchange_cols(shares)
    gram, *parts = together(sum_over_cols(gram), *parts)
    two_inverse = inverse_factor(gram)
    three = apply_factor(sum_cols(parts), two_inverse)
    three_inverse = inverse_factor(sum_everywhere(gram_of(three)))
    return (
        apply_factor(three, three_inverse) * factor,
        apply_factor(one, one_inverse) * factor,
        apply_factor(two, two_inverse) * factor,
    )


def solution(mesh):
    mesh = Mesh(mesh.devices.reshape([SIZE[name] for name in AXES]), AXES)
    rows, cols = ("y", "z"), ("x", "core")
    return jax.shard_map(
        on_device,
        mesh=mesh,
        in_specs=(P(AXES, None), P(rows, cols, None, None, None), P(rows, cols, None, None)),
        out_specs=(P(AXES, None),) * 3,
        check_vma=False,
    )
```

```python
import functools
import math

import jax
import jax.numpy as jnp
from jax import lax
from jax.experimental import pallas as pl
from jax.experimental.pallas import tpu as pltpu
from jax.sharding import Mesh, PartitionSpec as P

highest = lax.Precision.HIGHEST
f32 = jnp.float32
bf16 = jnp.bfloat16
AXES = ("y", "z", "x", "core")
SIZE = {"y": 4, "z": 8, "x": 4, "core": 2}
GROUP = 4
BLOCK = 64
PIVOTS = 16
TAIL = 16
LEVELS = 16383.0
CHUNK = 128
MIB = 1024 * 1024
GIGA = 1000**3


def send(value, axis, step):
    size = SIZE[axis]
    return lax.ppermute(value, axis, [(i, (i + step) % size) for i in range(size)])


def ring_gather(piece, axis):
    size = SIZE[axis]
    half = size // 2
    cut = piece.shape[0] // 2
    got = {0: piece}
    down = up = piece
    for k in range(1, half):
        down = send(down, axis, -1)
        up = send(up, axis, 1)
        got[k], got[size - k] = down, up
    first = send(down[:cut], axis, -1)
    second = send(up[cut:], axis, 1)
    return [got[k] for k in range(half)] + [first, second] + [got[k] for k in range(half + 1, size)]


def largest(value):
    return jnp.max(jnp.abs(value), axis=-2, keepdims=True)


def power_of(bound):
    power = jnp.clip(jnp.ceil(jnp.log2(jnp.maximum(bound, 1e-36))), -119, 119)
    return power, jnp.exp2(-power) * LEVELS


def encode(value, bound):
    power, scale = power_of(bound)
    whole = jnp.round(value * scale).astype(jnp.int16)
    tail = jnp.broadcast_to(power.astype(jnp.int16), value.shape[:-2] + (TAIL, value.shape[-1]))
    return jnp.concatenate([whole, tail], axis=-2)


def decode(message):
    bound = jnp.exp2(message[..., -1:, :].astype(f32))
    return message[..., :-TAIL, :].astype(f32) * (bound * (1 / LEVELS)), bound


def together(*values):
    return lax.optimization_barrier(values)


def whole(value):
    return jnp.round(value).astype(jnp.int32).astype(jnp.int16)


def relay_kernel(first, part_ref, bound_ref, message_ref, out_ref):
    rows = part_ref.shape[0]
    arrived = message_ref.shape[0] - TAIL
    bound = jnp.exp2(message_ref[arrived:, :].astype(jnp.int32).astype(f32)[:1])
    power, scale = power_of(bound_ref[...] + bound)
    step = bound * (1 / LEVELS)

    def add(i, carry):
        here = pl.ds(pl.multiple_of(i * CHUNK, CHUNK), CHUNK)
        there = pl.ds(pl.multiple_of(first + i * CHUNK, CHUNK), CHUNK)
        value = part_ref[there, :] + message_ref[here, :].astype(jnp.int32).astype(f32) * step
        out_ref[there, :] = whole(value * scale)
        return carry

    def keep(i, carry):
        there = pl.ds(pl.multiple_of(arrived - first + i * CHUNK, CHUNK), CHUNK)
        out_ref[there, :] = whole(part_ref[there, :] * scale)
        return carry

    lax.fori_loop(0, arrived // CHUNK, add, 0)
    lax.fori_loop(0, (rows - arrived) // CHUNK, keep, 0)
    out_ref[rows:, :] = jnp.broadcast_to(power, (TAIL, power.shape[1])).astype(jnp.int32).astype(jnp.int16)


def relay(first, part, bound, message):
    return pl.pallas_call(
        functools.partial(relay_kernel, first),
        out_shape=jax.ShapeDtypeStruct((part.shape[0] + TAIL, part.shape[1]), jnp.int16),
        compiler_params=pltpu.CompilerParams(vmem_limit_bytes=24 * MIB),
        cost_estimate=pl.CostEstimate(flops=0, bytes_accessed=8 * part.size, transcendentals=0),
    )(part, bound, message)


def settle_kernel(near_ref, up_ref, down_ref, out_ref, total):
    count, rows = out_ref.shape[0], out_ref.shape[1] - TAIL
    size = near_ref.shape[0]
    up_step = jnp.exp2(up_ref[size:, :].astype(jnp.int32).astype(f32)[:1]) * (1 / LEVELS)
    down_step = jnp.exp2(down_ref[size:, :].astype(jnp.int32).astype(f32)[:1]) * (1 / LEVELS)

    def group(k, carry):
        bound = jnp.zeros(up_step.shape, f32)
        for start in range(0, rows, CHUNK):
            here = pl.ds(pl.multiple_of(k * rows + start, CHUNK), CHUNK)
            value = near_ref[here, :] + up_ref[here, :].astype(jnp.int32).astype(f32) * up_step
            value = value + down_ref[here, :].astype(jnp.int32).astype(f32) * down_step
            total[start : start + CHUNK, :] = value
            bound = jnp.maximum(bound, jnp.max(jnp.abs(value), axis=0, keepdims=True))
        power, scale = power_of(bound)
        out_ref[k, :rows, :] = whole(total[...] * scale)
        out_ref[k, rows:, :] = jnp.broadcast_to(power, (TAIL, power.shape[1])).astype(jnp.int32).astype(jnp.int16)
        return carry

    lax.fori_loop(0, count, group, 0)


def settle(near, up, down, count):
    rows, width = near.shape[0] // count, near.shape[1]
    return pl.pallas_call(
        settle_kernel,
        out_shape=jax.ShapeDtypeStruct((count, rows + TAIL, width), jnp.int16),
        scratch_shapes=[pltpu.VMEM((rows, width), f32)],
        compiler_params=pltpu.CompilerParams(vmem_limit_bytes=24 * MIB),
        cost_estimate=pl.CostEstimate(flops=0, bytes_accessed=10 * near.size, transcendentals=0),
    )(near, up, down)


def direct_gather(piece, axis):
    size = SIZE[axis]
    return [piece] + [send(piece, axis, -k if k <= size // 2 else size - k) for k in range(1, size)]


def gather_rows(panel):
    tile = panel.shape[0] // 2
    two = jnp.concatenate(direct_gather(panel[tile:], "y"))
    one = jnp.broadcast_to(panel[:tile], (8, tile, panel.shape[1])).reshape(8 * tile, -1)
    one = lax.all_to_all(one, "z", split_axis=0, concat_axis=0, tiled=True)
    return ring_gather(one, "y"), ring_gather(two, "z")


def sum_rows(first, second, shares, gram):
    near, _, up, up_bound, down, down_bound = shares
    cut = near.shape[0] // 2
    up = send(relay(0, up, up_bound, first), "y", 1)
    down = send(relay(cut, down, down_bound, second), "y", -1)
    gram = sum_along_z(gram_over_x(gram))
    up, down, gram = together(up, down, gram)
    messages = settle(near, up, down, 8)
    rows = messages.shape[1]
    messages = lax.all_to_all(messages.reshape(8 * rows, -1), "z", split_axis=0, concat_axis=0, tiled=True)
    inverse = inverse_factor(gram_back(sum_direct(gram, "y")))
    messages, inverse = together(messages, inverse)
    return jnp.sum(decode(messages.reshape(8, rows, -1))[0], axis=0), inverse


def gather_cols(panel):
    near = jnp.concatenate(ring_gather(panel, "x"))
    return [near, send(near, "core", 1)]


def exchange_cols(shares):
    near, _, far, _ = shares
    both = (near + send(far, "core", 1)).reshape(4, -1, near.shape[1])
    messages = encode(both, largest(both))
    return [both[0]] + [send(messages[k], "x", k if k < 3 else -1) for k in range(1, 4)]


def sum_cols(parts):
    return functools.reduce(jnp.add, [decode(message)[0] for message in parts[1:]], parts[0])


def sum_direct(value, axis):
    size = SIZE[axis]
    moved = [send(value, axis, k if k <= size // 2 else k - size) for k in range(1, size)]
    return functools.reduce(jnp.add, moved, value)


def sum_flipped(value, axis, flips):
    moved = [lax.ppermute(value, axis, [(i, i ^ flip) for i in range(SIZE[axis])]) for flip in flips]
    return functools.reduce(jnp.add, moved, value)


def sum_parts(gram, axes, count):
    parts = lax.all_to_all(gram, axes, split_axis=0, concat_axis=0, tiled=True)
    return jnp.sum(parts.reshape(count, -1, gram.shape[1]), axis=0)


def spread(part, axes, count):
    copies = jnp.broadcast_to(part, (count,) + part.shape).reshape(-1, part.shape[1])
    return lax.all_to_all(copies, axes, split_axis=0, concat_axis=0, tiled=True)


def sum_everywhere(gram):
    part = sum_parts(gram, ("y", "x", "core"), 32)
    part = jnp.sum(spread(part, "z", 8).reshape((8,) + part.shape), axis=0)
    return spread(part, ("y", "x", "core"), 32)


def gram_over_core(gram):
    core = lax.axis_index("core")
    quads = gram.reshape(2, 4, -1, gram.shape[1])
    mine = lax.dynamic_index_in_dim(quads, core, 0, keepdims=False)
    theirs = lax.dynamic_index_in_dim(quads, 1 - core, 0, keepdims=False)
    return mine + send(theirs, "core", 1)


def gram_over_x(mine):
    place = lax.axis_index("x")

    def pick(k):
        return lax.dynamic_index_in_dim(mine, lax.rem(place + k, 4), 0, keepdims=False)

    return pick(0) + send(pick(1), "x", 1) + send(pick(2), "x", 2) + send(pick(3), "x", -1)


def sum_along_z(part):
    return sum_flipped(sum_flipped(part, "z", (1, 2, 3)), "z", (4,))


def gram_back(part):
    core = lax.axis_index("core")
    place = lax.axis_index("x")
    got = jnp.stack([part, send(part, "x", -1), send(part, "x", 2), send(part, "x", 1)])
    back = jnp.stack(
        [lax.dynamic_index_in_dim(got, lax.rem(k - place + 4, 4), 0, keepdims=False) for k in range(4)]
    )
    other = send(back, "core", 1)
    both = jnp.where(core == 0, jnp.stack([back, other]), jnp.stack([other, back]))
    return both.reshape(-1, part.shape[1])


def sum_over_cols(gram):
    core = lax.axis_index("core")
    halves = gram.reshape(2, -1, gram.shape[1])
    mine = lax.dynamic_index_in_dim(halves, core, 0, keepdims=False)
    theirs = lax.dynamic_index_in_dim(halves, 1 - core, 0, keepdims=False)
    mine = sum_direct(mine + send(theirs, "core", 1), "x")
    other = send(mine, "core", 1)
    return jnp.where(core == 0, jnp.stack([mine, other]), jnp.stack([other, mine])).reshape(gram.shape)


def product_kernel(transpose, spans, low, source_low, plain, coded, with_gram, begun, count_ref, to_ref, from_ref, tiles, *rest):
    pieces, rest = rest[: len(spans)], rest[len(spans) :]
    before, rest = rest[:begun], rest[begun:]
    outs, rest = rest[: 2 * len(plain) + len(coded) + with_gram], rest[2 * len(plain) + len(coded) + with_gram :]
    held, tiles_ref, total, slots, places, sources, arrived, left = rest
    copies = [
        pltpu.make_async_copy(piece, held.at[pl.ds(start, length)], arrived.at[i])
        for i, (piece, (start, length)) in enumerate(zip(pieces, spans))
    ]
    copies.append(pltpu.make_async_copy(tiles, tiles_ref, arrived.at[len(pieces)]))
    blocks_here = sum(plain) + sum(coded)
    if begun:
        start = 0
        for k, blocks in enumerate(plain):
            copies.append(
                pltpu.make_async_copy(
                    before[k], total.at[pl.ds(start, blocks)], arrived.at[len(pieces) + 1 + k]
                )
            )
            start += blocks
    for copy in copies:
        copy.start()
    if not begun:
        total[...] = jnp.zeros_like(total)

    def choose(i, found):
        place = to_ref[i] - low
        source = from_ref[i] - source_low
        slots[found] = i
        places[found] = place
        sources[found] = source
        inside = (place >= 0) & (place < blocks_here) & (source >= 0) & (source < held.shape[0])
        return found + jnp.where(inside, 1, 0)

    found = lax.fori_loop(0, count_ref[0], choose, 0)
    for j in range(GROUP):
        slots[found + j] = 0
        places[found + j] = blocks_here
        sources[found + j] = 0
    for copy in copies:
        copy.wait()
    dims = (((0,), (0,)), ((), ())) if transpose else (((1,), (0,)), ((), ()))

    def step(i, carry):
        products = []
        for j in range(GROUP):
            slot = slots[i * GROUP + j]
            block = held[sources[i * GROUP + j]]
            products.append(lax.dot_general(tiles_ref[slot], block, dims, preferred_element_type=f32))
        for j in range(GROUP):
            total[places[i * GROUP + j]] += products[j]
        return carry

    lax.fori_loop(0, (found + GROUP - 1) // GROUP, step, 0)
    start = 0
    copies = []
    for k, blocks in enumerate(plain):
        copies.append(pltpu.make_async_copy(total.at[pl.ds(start, blocks)], outs[2 * k], left.at[k]))
        copies[-1].start()
        start += blocks

    def bound_of(start, blocks):
        def widen(i, bound):
            return jnp.maximum(bound, jnp.max(jnp.abs(total[start + i]), axis=0, keepdims=True))

        return lax.fori_loop(0, blocks, widen, jnp.zeros((1, total.shape[2]), f32))

    start = 0
    for k, blocks in enumerate(plain):
        bound_ref = outs[2 * k + 1]
        if transpose and k:
            bound_ref[...] = bound_of(start, blocks)
        else:
            bound_ref[...] = jnp.zeros_like(bound_ref)
        start += blocks
    tile = total.shape[1]
    for k, blocks in enumerate(coded):
        out_ref = outs[2 * len(plain) + k]
        power, scale = power_of(bound_of(start, blocks))

        def finish(i, carry, out_ref=out_ref, start=start, scale=scale):
            rows = pl.ds(pl.multiple_of(i * tile, tile), tile)
            out_ref[rows, :] = whole(total[start + i] * scale)
            return carry

        lax.fori_loop(0, blocks, finish, 0)
        out_ref[blocks * tile :, :] = jnp.broadcast_to(power, (TAIL, power.shape[1])).astype(jnp.int32).astype(jnp.int16)
        start += blocks
    if with_gram:
        gram_ref = outs[-1]
        gram_ref[...] = before[-1][...] if begun else jnp.zeros_like(gram_ref)

        def add(i, carry):
            block = held[pl.ds(i * 8, 8)].reshape(8 * tile, -1)
            gram_ref[...] += lax.dot_general(block, block, (((0,), (0,)), ((), ())), preferred_element_type=f32)
            return carry

        lax.fori_loop(0, held.shape[0] // 8, add, 0)
    for copy in copies:
        copy.wait()


def product(
    tiles, pieces, to, source, count, low, plain, coded, transpose, with_gram=False, source_low=0, before=()
):
    slots, tile, _ = tiles.shape
    width = pieces[0].shape[1]
    pieces = [piece.reshape(-1, tile, width) for piece in pieces]
    spans, start = [], 0
    for piece in pieces:
        spans.append((start, piece.shape[0]))
        start += piece.shape[0]
    outs = sum(plain) + sum(coded)
    before = [x.reshape(-1, tile, width) for x in before[: 2 * len(plain) : 2]] + list(before[2 * len(plain) :])
    smem = pl.BlockSpec(memory_space=pltpu.SMEM)
    vmem = pl.BlockSpec(memory_space=pltpu.VMEM)
    shapes = []
    for blocks in plain:
        shapes += [jax.ShapeDtypeStruct((blocks, tile, width), f32), jax.ShapeDtypeStruct((1, width), f32)]
    shapes += [jax.ShapeDtypeStruct((blocks * tile + TAIL, width), jnp.int16) for blocks in coded]
    shapes += [jax.ShapeDtypeStruct((width, width), f32)] * with_gram
    found = pl.pallas_call(
        functools.partial(
            product_kernel, transpose, tuple(spans), low, source_low, plain, coded, with_gram, len(before)
        ),
        out_shape=shapes,
        in_specs=[smem, smem, smem]
        + [pl.BlockSpec(memory_space=pl.ANY)] * (1 + len(pieces) + min(len(before), len(plain)))
        + [vmem] * max(len(before) - len(plain), 0),
        out_specs=[pl.BlockSpec(memory_space=pl.ANY), vmem] * len(plain) + [vmem] * (len(coded) + with_gram),
        scratch_shapes=[
            pltpu.VMEM((start, tile, width), bf16),
            pltpu.VMEM((slots, tile, tile), bf16),
            pltpu.VMEM((outs + 1, tile, width), f32),
            pltpu.SMEM((slots + GROUP,), jnp.int32),
            pltpu.SMEM((slots + GROUP,), jnp.int32),
            pltpu.SMEM((slots + GROUP,), jnp.int32),
            pltpu.SemaphoreType.DMA((len(pieces) + 1 + len(plain),)),
            pltpu.SemaphoreType.DMA((max(len(plain), 1),)),
        ],
        compiler_params=pltpu.CompilerParams(vmem_limit_bytes=48 * MIB),
        cost_estimate=pl.CostEstimate(
            flops=2 * slots * tile * tile * width,
            bytes_accessed=2 * (slots * tile * tile + (start + 2 * outs) * tile * width),
            transcendentals=0,
        ),
    )(count, to, source, tiles, *pieces, *before)
    return [x.reshape(-1, width) for x in found]


def gram_of(panel):
    return lax.dot_general(panel, panel, (((0,), (0,)), ((), ())), precision=highest)


def apply_factor(panel, inverse):
    return lax.dot_general(panel, inverse, (((1,), (1,)), ((), ())), precision=highest)


def factor_kernel(gram_ref, out_ref, work):
    order = gram_ref.shape[0]
    shape = (BLOCK, 128)
    row_id = lax.broadcasted_iota(jnp.int32, shape, 0)
    unit = jnp.where(row_id == lax.broadcasted_iota(jnp.int32, shape, 1), 1.0, 0.0)
    work[:, :order] = gram_ref[...]
    square = (order, order)
    work[:, order:] = jnp.where(
        lax.broadcasted_iota(jnp.int32, square, 0) == lax.broadcasted_iota(jnp.int32, square, 1), 1.0, 0.0
    )
    for low in range(0, order, BLOCK):
        group = low // 128 * 128
        left = work[low : low + BLOCK, group : group + 128]
        right = unit
        pivots = jnp.ones(shape, f32)
        for start in range(0, BLOCK, PIVOTS):
            lane = low - group + start
            columns = [
                jnp.broadcast_to(left[:, lane + m : lane + m + 1], shape) for m in range(PIVOTS)
            ]
            for m in range(PIVOTS):
                at = start + m
                column = columns[m]
                pivot = jnp.broadcast_to(column[at : at + 1], shape)
                pivots = jnp.where(row_id == at, pivot, pivots)
                weight = jnp.where(row_id > at, column * (1.0 / pivot), 0.0)
                for q in range(m + 1, PIVOTS):
                    columns[q] = columns[q] - weight * column[start + q : start + q + 1]
                left = left - weight * left[at : at + 1]
                right = right - weight * right[at : at + 1]
        root = lax.rsqrt(pivots)
        root = root * (1.5 - 0.5 * pivots * root * root)
        right = right * root
        rows = jnp.dot(
            right[:, :BLOCK], work[low : low + BLOCK, :], precision=highest, preferred_element_type=f32
        )
        out_ref[low : low + BLOCK, :] = rows[:, order:]
        if low + BLOCK < order:
            update = lax.dot_general(
                rows[:, :order], rows, (((0,), (0,)), ((), ())), precision=highest, preferred_element_type=f32
            )
            work[low + BLOCK :, :] -= update[low + BLOCK :, :]


def inverse_factor(gram):
    order = gram.shape[0]
    return pl.pallas_call(
        factor_kernel,
        out_shape=jax.ShapeDtypeStruct(gram.shape, f32),
        scratch_shapes=[pltpu.VMEM((order, 2 * order), f32)],
        compiler_params=pltpu.CompilerParams(vmem_limit_bytes=16 * MIB),
        cost_estimate=pl.CostEstimate(flops=12 * GIGA, bytes_accessed=40 * MIB, transcendentals=0),
    )(gram)


def on_device(omega, tiles, coords):
    tile = tiles.shape[-1]
    factor = math.sqrt(omega.shape[0] * 256)
    local_tiles = tiles.reshape(tiles.shape[2], tile, tile)
    pairs = coords.reshape(coords.shape[2], 2)
    live = pairs[:, 0] >= 0
    count = jnp.sum(live.astype(jnp.int32)).reshape(1)
    my_y, my_z = lax.axis_index("y"), lax.axis_index("z")
    my_x, my_core = lax.axis_index("x"), lax.axis_index("core")

    local_row = jnp.clip(pairs[:, 0] - (my_y * 8 + my_z) * 16, 0, 15)
    keeper = local_row // 2
    row_slot = ((keeper + my_core) % 2 * 4 + (keeper // 2 - my_x + 4) % 4) * 2 + local_row % 2
    block_col = jnp.maximum(pairs[:, 1], 0)
    owner = block_col // 16
    far_y = (owner // 8 - my_y + 4) % 4
    far_z = (owner % 8 - my_z + 8) % 8
    panel_slot = jnp.where(block_col % 2 == 0, far_y * 8 + owner % 8, 32 + far_z * 4 + far_y)
    order_y = jnp.where(far_y == 2, 3, jnp.where(far_y == 3, 2, far_y))
    column_slot = (order_y * 8 + owner % 8) * 2 + block_col % 2
    row_to = jnp.where(live, row_slot, 16)
    column_to = jnp.where(live, column_slot, 64)

    def forward(panel, with_gram=False):
        ones, twos = gather_rows(panel.astype(bf16))

        def part(pieces, start, before=()):
            return product(
                local_tiles, pieces, row_to, panel_slot, count, 0, (8, 8), (), False, with_gram, start, before
            )

        return part(twos, 32, part(ones, 0))

    one = sum_cols(exchange_cols(forward(omega)))
    pieces = gather_cols(one.astype(bf16))
    far = product(local_tiles, pieces, column_to, row_slot, count, 48, (), (8, 8), True)
    *far, pieces[0], held_back = together(*far, pieces[0], one)
    first, second = send(far[0], "y", 1), send(far[1], "y", -1)
    shares = product(local_tiles, pieces, column_to, row_slot, count, 0, (16, 16, 16), (), True)
    gram = gram_over_core(gram_of(held_back))
    first, second, gram, *shares = together(first, second, gram, *shares)
    total, one_inverse = sum_rows(first, second, shares, gram)
    two = apply_factor(total, one_inverse)
    *shares, gram = forward(two, True)
    parts = exchange_cols(shares)
    gram, *parts = together(sum_over_cols(gram), *parts)
    two_inverse = inverse_factor(gram)
    three = apply_factor(sum_cols(parts), two_inverse)
    three_inverse = inverse_factor(sum_everywhere(gram_of(three)))
    return (
        apply_factor(three, three_inverse) * factor,
        apply_factor(one, one_inverse) * factor,
        apply_factor(two, two_inverse) * factor,
    )


def solution(mesh):
    mesh = Mesh(mesh.devices.reshape([SIZE[name] for name in AXES]), AXES)
    rows, cols = ("y", "z"), ("x", "core")
    return jax.shard_map(
        on_device,
        mesh=mesh,
        in_specs=(P(AXES, None), P(rows, cols, None, None, None), P(rows, cols, None, None)),
        out_specs=(P(AXES, None),) * 3,
        check_vma=False,
    )
```

```python
import functools
import math

import jax
import jax.numpy as jnp
from jax import lax
from jax.experimental import pallas as pl
from jax.experimental.pallas import tpu as pltpu
from jax.sharding import Mesh, PartitionSpec as P

highest = lax.Precision.HIGHEST
f32 = jnp.float32
bf16 = jnp.bfloat16
AXES = ("y", "z", "x", "core")
SIZE = {"y": 4, "z": 8, "x": 4, "core": 2}
GROUP = 4
BLOCK = 64
PIVOTS = 16
TAIL = 16
LEVELS = 16383.0
CHUNK = 128
MIB = 1024 * 1024
GIGA = 1000**3


def send(value, axis, step):
    size = SIZE[axis]
    return lax.ppermute(value, axis, [(i, (i + step) % size) for i in range(size)])


def ring_gather(piece, axis):
    size = SIZE[axis]
    half = size // 2
    cut = piece.shape[0] // 2
    got = {0: piece}
    down = up = piece
    for k in range(1, half):
        down = send(down, axis, -1)
        up = send(up, axis, 1)
        got[k], got[size - k] = down, up
    first = send(down[:cut], axis, -1)
    second = send(up[cut:], axis, 1)
    return [got[k] for k in range(half)] + [first, second] + [got[k] for k in range(half + 1, size)]


def largest(value):
    return jnp.max(jnp.abs(value), axis=-2, keepdims=True)


def power_of(bound):
    power = jnp.clip(jnp.ceil(jnp.log2(jnp.maximum(bound, 1e-36))), -119, 119)
    return power, jnp.exp2(-power) * LEVELS


def encode(value, bound):
    power, scale = power_of(bound)
    whole = jnp.round(value * scale).astype(jnp.int16)
    tail = jnp.broadcast_to(power.astype(jnp.int16), value.shape[:-2] + (TAIL, value.shape[-1]))
    return jnp.concatenate([whole, tail], axis=-2)


def decode(message):
    bound = jnp.exp2(message[..., -1:, :].astype(f32))
    return message[..., :-TAIL, :].astype(f32) * (bound * (1 / LEVELS)), bound


def together(*values):
    return lax.optimization_barrier(values)


def whole(value):
    return jnp.round(value).astype(jnp.int32).astype(jnp.int16)


def relay_kernel(first, part_ref, bound_ref, message_ref, out_ref):
    rows = part_ref.shape[0]
    arrived = message_ref.shape[0] - TAIL
    bound = jnp.exp2(message_ref[arrived:, :].astype(jnp.int32).astype(f32)[:1])
    power, scale = power_of(bound_ref[...] + bound)
    step = bound * (1 / LEVELS)

    def add(i, carry):
        here = pl.ds(pl.multiple_of(i * CHUNK, CHUNK), CHUNK)
        there = pl.ds(pl.multiple_of(first + i * CHUNK, CHUNK), CHUNK)
        value = part_ref[there, :] + message_ref[here, :].astype(jnp.int32).astype(f32) * step
        out_ref[there, :] = whole(value * scale)
        return carry

    def keep(i, carry):
        there = pl.ds(pl.multiple_of(arrived - first + i * CHUNK, CHUNK), CHUNK)
        out_ref[there, :] = whole(part_ref[there, :] * scale)
        return carry

    lax.fori_loop(0, arrived // CHUNK, add, 0)
    lax.fori_loop(0, (rows - arrived) // CHUNK, keep, 0)
    out_ref[rows:, :] = jnp.broadcast_to(power, (TAIL, power.shape[1])).astype(jnp.int32).astype(jnp.int16)


def relay(first, part, bound, message):
    return pl.pallas_call(
        functools.partial(relay_kernel, first),
        out_shape=jax.ShapeDtypeStruct((part.shape[0] + TAIL, part.shape[1]), jnp.int16),
        compiler_params=pltpu.CompilerParams(vmem_limit_bytes=24 * MIB),
        cost_estimate=pl.CostEstimate(flops=0, bytes_accessed=8 * part.size, transcendentals=0),
    )(part, bound, message)


def settle_kernel(near_ref, up_ref, down_ref, out_ref, total):
    count, rows = out_ref.shape[0], out_ref.shape[1] - TAIL
    size = near_ref.shape[0]
    up_step = jnp.exp2(up_ref[size:, :].astype(jnp.int32).astype(f32)[:1]) * (1 / LEVELS)
    down_step = jnp.exp2(down_ref[size:, :].astype(jnp.int32).astype(f32)[:1]) * (1 / LEVELS)

    def group(k, carry):
        bound = jnp.zeros(up_step.shape, f32)
        for start in range(0, rows, CHUNK):
            here = pl.ds(pl.multiple_of(k * rows + start, CHUNK), CHUNK)
            value = near_ref[here, :] + up_ref[here, :].astype(jnp.int32).astype(f32) * up_step
            value = value + down_ref[here, :].astype(jnp.int32).astype(f32) * down_step
            total[start : start + CHUNK, :] = value
            bound = jnp.maximum(bound, jnp.max(jnp.abs(value), axis=0, keepdims=True))
        power, scale = power_of(bound)
        out_ref[k, :rows, :] = whole(total[...] * scale)
        out_ref[k, rows:, :] = jnp.broadcast_to(power, (TAIL, power.shape[1])).astype(jnp.int32).astype(jnp.int16)
        return carry

    lax.fori_loop(0, count, group, 0)


def settle(near, up, down, count):
    rows, width = near.shape[0] // count, near.shape[1]
    return pl.pallas_call(
        settle_kernel,
        out_shape=jax.ShapeDtypeStruct((count, rows + TAIL, width), jnp.int16),
        scratch_shapes=[pltpu.VMEM((rows, width), f32)],
        compiler_params=pltpu.CompilerParams(vmem_limit_bytes=24 * MIB),
        cost_estimate=pl.CostEstimate(flops=0, bytes_accessed=10 * near.size, transcendentals=0),
    )(near, up, down)


def direct_gather(piece, axis):
    size = SIZE[axis]
    return [piece] + [send(piece, axis, -k if k <= size // 2 else size - k) for k in range(1, size)]


def gather_rows(panel):
    tile = panel.shape[0] // 2
    two = jnp.concatenate(direct_gather(panel[tile:], "y"))
    one = jnp.broadcast_to(panel[:tile], (8, tile, panel.shape[1])).reshape(8 * tile, -1)
    one = lax.all_to_all(one, "z", split_axis=0, concat_axis=0, tiled=True)
    return ring_gather(one, "y") + ring_gather(two, "z")


def sum_rows(came, shares, gram):
    near, up, up_bound = shares[0:3:2], shares[4:8:2], shares[5:8:2]
    down, down_bound = shares[8:12:2], shares[9:12:2]
    cut = near[0].shape[0] // 2
    ups, downs = [], []
    first, second = came[:2]
    for k in range(2):
        above, below = relay(0, up[k], up_bound[k], first), relay(cut, down[k], down_bound[k], second)
        first, second, *_ = together(*came[2:], above, below)
        ups.append(send(above, "y", 1))
        downs.append(send(below, "y", -1))
    gram = sum_along_z(gram_over_x(gram))
    sums = []
    for k in range(2):
        if k:
            ups[k], downs[k], gram, _ = together(ups[k], downs[k], gram, messages)
        messages = settle(near[k], ups[k], downs[k], 8)
        rows = messages.shape[1]
        messages = lax.all_to_all(messages.reshape(8 * rows, -1), "z", split_axis=0, concat_axis=0, tiled=True)
        sums.append(messages.reshape(8, rows, -1))
    inverse = inverse_factor(gram_back(sum_direct(gram, "y")))
    *sums, inverse = together(*sums, inverse)
    return jnp.concatenate([jnp.sum(decode(messages)[0], axis=0) for messages in sums]), inverse


def gather_cols(panel):
    near = jnp.concatenate(ring_gather(panel, "x"))
    return [near, send(near, "core", 1)]


def exchange_cols(shares):
    near, _, far, _ = shares
    both = (near + send(far, "core", 1)).reshape(4, -1, near.shape[1])
    messages = encode(both, largest(both))
    return [both[0]] + [send(messages[k], "x", k if k < 3 else -1) for k in range(1, 4)]


def sum_cols(parts):
    return functools.reduce(jnp.add, [decode(message)[0] for message in parts[1:]], parts[0])


def sum_direct(value, axis):
    size = SIZE[axis]
    moved = [send(value, axis, k if k <= size // 2 else k - size) for k in range(1, size)]
    return functools.reduce(jnp.add, moved, value)


def sum_flipped(value, axis, flips):
    moved = [lax.ppermute(value, axis, [(i, i ^ flip) for i in range(SIZE[axis])]) for flip in flips]
    return functools.reduce(jnp.add, moved, value)


def sum_parts(gram, axes, count):
    parts = lax.all_to_all(gram, axes, split_axis=0, concat_axis=0, tiled=True)
    return jnp.sum(parts.reshape(count, -1, gram.shape[1]), axis=0)


def spread(part, axes, count):
    copies = jnp.broadcast_to(part, (count,) + part.shape).reshape(-1, part.shape[1])
    return lax.all_to_all(copies, axes, split_axis=0, concat_axis=0, tiled=True)


def sum_everywhere(gram):
    part = sum_parts(gram, ("y", "x", "core"), 32)
    part = jnp.sum(spread(part, "z", 8).reshape((8,) + part.shape), axis=0)
    return spread(part, ("y", "x", "core"), 32)


def gram_over_core(gram):
    core = lax.axis_index("core")
    quads = gram.reshape(2, 4, -1, gram.shape[1])
    mine = lax.dynamic_index_in_dim(quads, core, 0, keepdims=False)
    theirs = lax.dynamic_index_in_dim(quads, 1 - core, 0, keepdims=False)
    return mine + send(theirs, "core", 1)


def gram_over_x(mine):
    place = lax.axis_index("x")

    def pick(k):
        return lax.dynamic_index_in_dim(mine, lax.rem(place + k, 4), 0, keepdims=False)

    return pick(0) + send(pick(1), "x", 1) + send(pick(2), "x", 2) + send(pick(3), "x", -1)


def sum_along_z(part):
    return sum_flipped(sum_flipped(part, "z", (1, 2, 3)), "z", (4,))


def gram_back(part):
    core = lax.axis_index("core")
    place = lax.axis_index("x")
    got = jnp.stack([part, send(part, "x", -1), send(part, "x", 2), send(part, "x", 1)])
    back = jnp.stack(
        [lax.dynamic_index_in_dim(got, lax.rem(k - place + 4, 4), 0, keepdims=False) for k in range(4)]
    )
    other = send(back, "core", 1)
    both = jnp.where(core == 0, jnp.stack([back, other]), jnp.stack([other, back]))
    return both.reshape(-1, part.shape[1])


def sum_over_cols(gram):
    core = lax.axis_index("core")
    halves = gram.reshape(2, -1, gram.shape[1])
    mine = lax.dynamic_index_in_dim(halves, core, 0, keepdims=False)
    theirs = lax.dynamic_index_in_dim(halves, 1 - core, 0, keepdims=False)
    mine = sum_direct(mine + send(theirs, "core", 1), "x")
    other = send(mine, "core", 1)
    return jnp.where(core == 0, jnp.stack([mine, other]), jnp.stack([other, mine])).reshape(gram.shape)


def product_kernel(transpose, spans, low, plain, coded, with_gram, count_ref, to_ref, from_ref, tiles, *rest):
    pieces, rest = rest[: len(spans)], rest[len(spans) :]
    outs, rest = rest[: 2 * len(plain) + len(coded) + with_gram], rest[2 * len(plain) + len(coded) + with_gram :]
    held, tiles_ref, total, slots, places, arrived, left = rest
    copies = [
        pltpu.make_async_copy(piece, held.at[pl.ds(start, length)], arrived.at[i])
        for i, (piece, (start, length)) in enumerate(zip(pieces, spans))
    ]
    copies.append(pltpu.make_async_copy(tiles, tiles_ref, arrived.at[len(pieces)]))
    for copy in copies:
        copy.start()
    total[...] = jnp.zeros_like(total)
    blocks_here = sum(plain) + sum(coded)

    def choose(i, found):
        place = to_ref[i] - low
        slots[found] = i
        places[found] = place
        return found + jnp.where((place >= 0) & (place < blocks_here), 1, 0)

    found = lax.fori_loop(0, count_ref[0], choose, 0)
    for j in range(GROUP):
        slots[found + j] = 0
        places[found + j] = blocks_here
    for copy in copies:
        copy.wait()
    dims = (((0,), (0,)), ((), ())) if transpose else (((1,), (0,)), ((), ()))

    def step(i, carry):
        products = []
        for j in range(GROUP):
            slot = slots[i * GROUP + j]
            products.append(
                lax.dot_general(tiles_ref[slot], held[from_ref[slot]], dims, preferred_element_type=f32)
            )
        for j in range(GROUP):
            total[places[i * GROUP + j]] += products[j]
        return carry

    lax.fori_loop(0, (found + GROUP - 1) // GROUP, step, 0)
    start = 0
    copies = []
    for k, blocks in enumerate(plain):
        copies.append(pltpu.make_async_copy(total.at[pl.ds(start, blocks)], outs[2 * k], left.at[k]))
        copies[-1].start()
        start += blocks

    def bound_of(start, blocks):
        def widen(i, bound):
            return jnp.maximum(bound, jnp.max(jnp.abs(total[start + i]), axis=0, keepdims=True))

        return lax.fori_loop(0, blocks, widen, jnp.zeros((1, total.shape[2]), f32))

    start = 0
    for k, blocks in enumerate(plain):
        bound_ref = outs[2 * k + 1]
        if transpose and k:
            bound_ref[...] = bound_of(start, blocks)
        else:
            bound_ref[...] = jnp.zeros_like(bound_ref)
        start += blocks
    tile = total.shape[1]
    for k, blocks in enumerate(coded):
        out_ref = outs[2 * len(plain) + k]
        power, scale = power_of(bound_of(start, blocks))

        def finish(i, carry, out_ref=out_ref, start=start, scale=scale):
            rows = pl.ds(pl.multiple_of(i * tile, tile), tile)
            out_ref[rows, :] = whole(total[start + i] * scale)
            return carry

        lax.fori_loop(0, blocks, finish, 0)
        out_ref[blocks * tile :, :] = jnp.broadcast_to(power, (TAIL, power.shape[1])).astype(jnp.int32).astype(jnp.int16)
        start += blocks
    if with_gram:
        gram_ref = outs[-1]
        gram_ref[...] = jnp.zeros_like(gram_ref)

        def add(i, carry):
            block = held[pl.ds(i * GROUP, GROUP)].reshape(GROUP * tile, -1)
            gram_ref[...] += lax.dot_general(block, block, (((0,), (0,)), ((), ())), preferred_element_type=f32)
            return carry

        lax.fori_loop(0, held.shape[0] // GROUP, add, 0)
    for copy in copies:
        copy.wait()


def product(tiles, pieces, to, source, count, low, plain, coded, transpose, with_gram=False):
    slots, tile, _ = tiles.shape
    width = pieces[0].shape[1]
    pieces = [piece.reshape(-1, tile, width) for piece in pieces]
    spans, start = [], 0
    for piece in pieces:
        spans.append((start, piece.shape[0]))
        start += piece.shape[0]
    outs = sum(plain) + sum(coded)
    smem = pl.BlockSpec(memory_space=pltpu.SMEM)
    vmem = pl.BlockSpec(memory_space=pltpu.VMEM)
    shapes = []
    for blocks in plain:
        shapes += [jax.ShapeDtypeStruct((blocks, tile, width), f32), jax.ShapeDtypeStruct((1, width), f32)]
    shapes += [jax.ShapeDtypeStruct((blocks * tile + TAIL, width), jnp.int16) for blocks in coded]
    shapes += [jax.ShapeDtypeStruct((width, width), f32)] * with_gram
    found = pl.pallas_call(
        functools.partial(product_kernel, transpose, tuple(spans), low, plain, coded, with_gram),
        out_shape=shapes,
        in_specs=[smem, smem, smem] + [pl.BlockSpec(memory_space=pl.ANY)] * (1 + len(pieces)),
        out_specs=[pl.BlockSpec(memory_space=pl.ANY), vmem] * len(plain) + [vmem] * (len(coded) + with_gram),
        scratch_shapes=[
            pltpu.VMEM((start, tile, width), bf16),
            pltpu.VMEM((slots, tile, tile), bf16),
            pltpu.VMEM((outs + 1, tile, width), f32),
            pltpu.SMEM((slots + GROUP,), jnp.int32),
            pltpu.SMEM((slots + GROUP,), jnp.int32),
            pltpu.SemaphoreType.DMA((len(pieces) + 1,)),
            pltpu.SemaphoreType.DMA((max(len(plain), 1),)),
        ],
        compiler_params=pltpu.CompilerParams(vmem_limit_bytes=48 * MIB),
        cost_estimate=pl.CostEstimate(
            flops=2 * slots * tile * tile * width,
            bytes_accessed=2 * (slots * tile * tile + (start + 2 * outs) * tile * width),
            transcendentals=0,
        ),
    )(count, to, source, tiles, *pieces)
    return [x.reshape(-1, width) for x in found]


def gram_of(panel):
    return lax.dot_general(panel, panel, (((0,), (0,)), ((), ())), precision=highest)


def apply_factor(panel, inverse):
    return lax.dot_general(panel, inverse, (((1,), (1,)), ((), ())), precision=highest)


def factor_kernel(gram_ref, out_ref, work):
    order = gram_ref.shape[0]
    shape = (BLOCK, 128)
    row_id = lax.broadcasted_iota(jnp.int32, shape, 0)
    unit = jnp.where(row_id == lax.broadcasted_iota(jnp.int32, shape, 1), 1.0, 0.0)
    work[:, :order] = gram_ref[...]
    square = (order, order)
    work[:, order:] = jnp.where(
        lax.broadcasted_iota(jnp.int32, square, 0) == lax.broadcasted_iota(jnp.int32, square, 1), 1.0, 0.0
    )
    for low in range(0, order, BLOCK):
        group = low // 128 * 128
        left = work[low : low + BLOCK, group : group + 128]
        right = unit
        pivots = jnp.ones(shape, f32)
        for start in range(0, BLOCK, PIVOTS):
            lane = low - group + start
            columns = [
                jnp.broadcast_to(left[:, lane + m : lane + m + 1], shape) for m in range(PIVOTS)
            ]
            for m in range(PIVOTS):
                at = start + m
                column = columns[m]
                pivot = jnp.broadcast_to(column[at : at + 1], shape)
                pivots = jnp.where(row_id == at, pivot, pivots)
                weight = jnp.where(row_id > at, column * (1.0 / pivot), 0.0)
                for q in range(m + 1, PIVOTS):
                    columns[q] = columns[q] - weight * column[start + q : start + q + 1]
                left = left - weight * left[at : at + 1]
                right = right - weight * right[at : at + 1]
        root = lax.rsqrt(pivots)
        root = root * (1.5 - 0.5 * pivots * root * root)
        right = right * root
        rows = jnp.dot(
            right[:, :BLOCK], work[low : low + BLOCK, :], precision=highest, preferred_element_type=f32
        )
        out_ref[low : low + BLOCK, :] = rows[:, order:]
        if low + BLOCK < order:
            update = lax.dot_general(
                rows[:, :order], rows, (((0,), (0,)), ((), ())), precision=highest, preferred_element_type=f32
            )
            work[low + BLOCK :, :] -= update[low + BLOCK :, :]


def inverse_factor(gram):
    order = gram.shape[0]
    return pl.pallas_call(
        factor_kernel,
        out_shape=jax.ShapeDtypeStruct(gram.shape, f32),
        scratch_shapes=[pltpu.VMEM((order, 2 * order), f32)],
        compiler_params=pltpu.CompilerParams(vmem_limit_bytes=16 * MIB),
        cost_estimate=pl.CostEstimate(flops=12 * GIGA, bytes_accessed=40 * MIB, transcendentals=0),
    )(gram)


def on_device(omega, tiles, coords):
    tile = tiles.shape[-1]
    factor = math.sqrt(omega.shape[0] * 256)
    local_tiles = tiles.reshape(tiles.shape[2], tile, tile)
    pairs = coords.reshape(coords.shape[2], 2)
    live = pairs[:, 0] >= 0
    count = jnp.sum(live.astype(jnp.int32)).reshape(1)
    my_y, my_z = lax.axis_index("y"), lax.axis_index("z")
    my_x, my_core = lax.axis_index("x"), lax.axis_index("core")

    local_row = jnp.clip(pairs[:, 0] - (my_y * 8 + my_z) * 16, 0, 15)
    keeper = local_row // 2
    row_slot = ((keeper + my_core) % 2 * 4 + (keeper // 2 - my_x + 4) % 4) * 2 + local_row % 2
    block_col = jnp.maximum(pairs[:, 1], 0)
    owner = block_col // 16
    far_y = (owner // 8 - my_y + 4) % 4
    far_z = (owner % 8 - my_z + 8) % 8
    panel_slot = jnp.where(block_col % 2 == 0, far_y * 8 + owner % 8, 32 + far_z * 4 + far_y)
    order_y = jnp.where(far_y == 2, 3, jnp.where(far_y == 3, 2, far_y))
    column_slot = (order_y * 2 + block_col % 2) * 8 + owner % 8
    row_to = jnp.where(live, row_slot, 16)
    column_to = jnp.where(live, column_slot, 64)

    def forward(panel, with_gram=False):
        pieces = gather_rows(panel.astype(bf16))
        return product(local_tiles, pieces, row_to, panel_slot, count, 0, (8, 8), (), False, with_gram)

    one = sum_cols(exchange_cols(forward(omega)))
    pieces = gather_cols(one.astype(bf16))
    far = product(local_tiles, pieces, column_to, row_slot, count, 48, (), (4,) * 4, True)
    *far, pieces[0], held_back = together(*far, pieces[0], one)
    came = [send(message, "y", 1 - k % 2 * 2) for k, message in enumerate(far)]
    shares = product(local_tiles, pieces, column_to, row_slot, count, 0, (8,) * 6, (), True)
    gram = gram_over_core(gram_of(held_back))
    came[0], came[1], gram, *shares = together(came[0], came[1], gram, *shares)
    total, one_inverse = sum_rows(came, shares, gram)
    two = apply_factor(total, one_inverse)
    *shares, gram = forward(two, True)
    parts = exchange_cols(shares)
    gram, *parts = together(sum_over_cols(gram), *parts)
    two_inverse = inverse_factor(gram)
    three = apply_factor(sum_cols(parts), two_inverse)
    three_inverse = inverse_factor(sum_everywhere(gram_of(three)))
    return (
        apply_factor(three, three_inverse) * factor,
        apply_factor(one, one_inverse) * factor,
        apply_factor(two, two_inverse) * factor,
    )


def solution(mesh):
    mesh = Mesh(mesh.devices.reshape([SIZE[name] for name in AXES]), AXES)
    rows, cols = ("y", "z"), ("x", "core")
    return jax.shard_map(
        on_device,
        mesh=mesh,
        in_specs=(P(AXES, None), P(rows, cols, None, None, None), P(rows, cols, None, None)),
        out_specs=(P(AXES, None),) * 3,
        check_vma=False,
    )
```

```python
import functools
import math

import jax
import jax.numpy as jnp
from jax import lax
from jax.experimental import pallas as pl
from jax.experimental.pallas import tpu as pltpu
from jax.sharding import Mesh, PartitionSpec as P

highest = lax.Precision.HIGHEST
f32 = jnp.float32
bf16 = jnp.bfloat16
AXES = ("y", "z", "x", "core")
SIZE = {"y": 4, "z": 8, "x": 4, "core": 2}
GROUP = 4
BLOCK = 64
PIVOTS = 16
TAIL = 16
LEVELS = 16383.0
CHUNK = 128
MIB = 1024 * 1024
GIGA = 1000**3


def send(value, axis, step):
    size = SIZE[axis]
    return lax.ppermute(value, axis, [(i, (i + step) % size) for i in range(size)])


def ring_gather(piece, axis):
    size = SIZE[axis]
    half = size // 2
    cut = piece.shape[0] // 2
    got = {0: piece}
    down = up = piece
    for k in range(1, half):
        down = send(down, axis, -1)
        up = send(up, axis, 1)
        got[k], got[size - k] = down, up
    first = send(down[:cut], axis, -1)
    second = send(up[cut:], axis, 1)
    return [got[k] for k in range(half)] + [first, second] + [got[k] for k in range(half + 1, size)]


def largest(value):
    return jnp.max(jnp.abs(value), axis=-2, keepdims=True)


def power_of(bound):
    power = jnp.clip(jnp.ceil(jnp.log2(jnp.maximum(bound, 1e-36))), -119, 119)
    return power, jnp.exp2(-power) * LEVELS


def encode(value, bound):
    power, scale = power_of(bound)
    whole = jnp.round(value * scale).astype(jnp.int16)
    tail = jnp.broadcast_to(power.astype(jnp.int16), value.shape[:-2] + (TAIL, value.shape[-1]))
    return jnp.concatenate([whole, tail], axis=-2)


def decode(message):
    bound = jnp.exp2(message[..., -1:, :].astype(f32))
    return message[..., :-TAIL, :].astype(f32) * (bound * (1 / LEVELS)), bound


def together(*values):
    return lax.optimization_barrier(values)


def whole(value):
    return jnp.round(value).astype(jnp.int32).astype(jnp.int16)


def relay_kernel(first, part_ref, bound_ref, message_ref, out_ref):
    rows = part_ref.shape[0]
    arrived = message_ref.shape[0] - TAIL
    bound = jnp.exp2(message_ref[arrived:, :].astype(jnp.int32).astype(f32)[:1])
    power, scale = power_of(bound_ref[...] + bound)
    step = bound * (1 / LEVELS)

    def add(i, carry):
        here = pl.ds(pl.multiple_of(i * CHUNK, CHUNK), CHUNK)
        there = pl.ds(pl.multiple_of(first + i * CHUNK, CHUNK), CHUNK)
        value = part_ref[there, :] + message_ref[here, :].astype(jnp.int32).astype(f32) * step
        out_ref[there, :] = whole(value * scale)
        return carry

    def keep(i, carry):
        there = pl.ds(pl.multiple_of(arrived - first + i * CHUNK, CHUNK), CHUNK)
        out_ref[there, :] = whole(part_ref[there, :] * scale)
        return carry

    lax.fori_loop(0, arrived // CHUNK, add, 0)
    lax.fori_loop(0, (rows - arrived) // CHUNK, keep, 0)
    out_ref[rows:, :] = jnp.broadcast_to(power, (TAIL, power.shape[1])).astype(jnp.int32).astype(jnp.int16)


def relay(first, part, bound, message):
    return pl.pallas_call(
        functools.partial(relay_kernel, first),
        out_shape=jax.ShapeDtypeStruct((part.shape[0] + TAIL, part.shape[1]), jnp.int16),
        compiler_params=pltpu.CompilerParams(vmem_limit_bytes=24 * MIB),
        cost_estimate=pl.CostEstimate(flops=0, bytes_accessed=8 * part.size, transcendentals=0),
    )(part, bound, message)


def settle_kernel(near_ref, up_ref, down_ref, out_ref, total):
    count, rows = out_ref.shape[0], out_ref.shape[1] - TAIL
    size = near_ref.shape[0]
    up_step = jnp.exp2(up_ref[size:, :].astype(jnp.int32).astype(f32)[:1]) * (1 / LEVELS)
    down_step = jnp.exp2(down_ref[size:, :].astype(jnp.int32).astype(f32)[:1]) * (1 / LEVELS)

    def group(k, carry):
        bound = jnp.zeros(up_step.shape, f32)
        for start in range(0, rows, CHUNK):
            here = pl.ds(pl.multiple_of(k * rows + start, CHUNK), CHUNK)
            value = near_ref[here, :] + up_ref[here, :].astype(jnp.int32).astype(f32) * up_step
            value = value + down_ref[here, :].astype(jnp.int32).astype(f32) * down_step
            total[start : start + CHUNK, :] = value
            bound = jnp.maximum(bound, jnp.max(jnp.abs(value), axis=0, keepdims=True))
        power, scale = power_of(bound)
        out_ref[k, :rows, :] = whole(total[...] * scale)
        out_ref[k, rows:, :] = jnp.broadcast_to(power, (TAIL, power.shape[1])).astype(jnp.int32).astype(jnp.int16)
        return carry

    lax.fori_loop(0, count, group, 0)


def settle(near, up, down, count):
    rows, width = near.shape[0] // count, near.shape[1]
    return pl.pallas_call(
        settle_kernel,
        out_shape=jax.ShapeDtypeStruct((count, rows + TAIL, width), jnp.int16),
        scratch_shapes=[pltpu.VMEM((rows, width), f32)],
        compiler_params=pltpu.CompilerParams(vmem_limit_bytes=24 * MIB),
        cost_estimate=pl.CostEstimate(flops=0, bytes_accessed=10 * near.size, transcendentals=0),
    )(near, up, down)


def direct_gather(piece, axis):
    size = SIZE[axis]
    return [piece] + [send(piece, axis, -k if k <= size // 2 else size - k) for k in range(1, size)]


def gather_rows(panel):
    tile = panel.shape[0] // 2
    two = jnp.concatenate(direct_gather(panel[tile:], "y"))
    one = jnp.broadcast_to(panel[:tile], (8, tile, panel.shape[1])).reshape(8 * tile, -1)
    one = lax.all_to_all(one, "z", split_axis=0, concat_axis=0, tiled=True)
    return ring_gather(one, "y") + ring_gather(two, "z")


def sum_rows(first, second, shares, gram):
    near, _, up, up_bound, down, down_bound = shares
    cut = near.shape[0] // 2
    up = send(relay(0, up, up_bound, first), "y", 1)
    down = send(relay(cut, down, down_bound, second), "y", -1)
    gram = sum_along_z(gram_over_x(gram))
    up, down, gram = together(up, down, gram)
    messages = settle(near, up, down, 8)
    rows = messages.shape[1]
    messages = lax.all_to_all(messages.reshape(8 * rows, -1), "z", split_axis=0, concat_axis=0, tiled=True)
    inverse = inverse_factor(gram_back(sum_direct(gram, "y")))
    messages, inverse = together(messages, inverse)
    return jnp.sum(decode(messages.reshape(8, rows, -1))[0], axis=0), inverse


def gather_cols(panel):
    near = jnp.concatenate(ring_gather(panel, "x"))
    return [near, send(near, "core", 1)]


def exchange_cols(shares):
    near, _, far, _ = shares
    both = (near + send(far, "core", 1)).reshape(4, -1, near.shape[1])
    messages = encode(both, largest(both))
    return [both[0]] + [send(messages[k], "x", k if k < 3 else -1) for k in range(1, 4)]


def sum_cols(parts):
    return functools.reduce(jnp.add, [decode(message)[0] for message in parts[1:]], parts[0])


def sum_direct(value, axis):
    size = SIZE[axis]
    moved = [send(value, axis, k if k <= size // 2 else k - size) for k in range(1, size)]
    return functools.reduce(jnp.add, moved, value)


def sum_flipped(value, axis, flips):
    moved = [lax.ppermute(value, axis, [(i, i ^ flip) for i in range(SIZE[axis])]) for flip in flips]
    return functools.reduce(jnp.add, moved, value)


def sum_parts(gram, axes, count):
    parts = lax.all_to_all(gram, axes, split_axis=0, concat_axis=0, tiled=True)
    return jnp.sum(parts.reshape(count, -1, gram.shape[1]), axis=0)


def spread(part, axes, count):
    copies = jnp.broadcast_to(part, (count,) + part.shape).reshape(-1, part.shape[1])
    return lax.all_to_all(copies, axes, split_axis=0, concat_axis=0, tiled=True)


def sum_everywhere(gram):
    part = sum_parts(gram, ("y", "x", "core"), 32)
    part = jnp.sum(spread(part, "z", 8).reshape((8,) + part.shape), axis=0)
    return spread(part, ("y", "x", "core"), 32)


def largest_everywhere(value):
    for axes, count in ((("y", "x", "core"), 32), ("z", 8)):
        value = jnp.max(spread(jnp.full((8, 128), value), axes, count))
    return value


def gram_over_core(gram):
    core = lax.axis_index("core")
    quads = gram.reshape(2, 4, -1, gram.shape[1])
    mine = lax.dynamic_index_in_dim(quads, core, 0, keepdims=False)
    theirs = lax.dynamic_index_in_dim(quads, 1 - core, 0, keepdims=False)
    return mine + send(theirs, "core", 1)


def gram_over_x(mine):
    place = lax.axis_index("x")

    def pick(k):
        return lax.dynamic_index_in_dim(mine, lax.rem(place + k, 4), 0, keepdims=False)

    return pick(0) + send(pick(1), "x", 1) + send(pick(2), "x", 2) + send(pick(3), "x", -1)


def sum_along_z(part):
    return sum_flipped(sum_flipped(part, "z", (1, 2, 3)), "z", (4,))


def gram_back(part):
    core = lax.axis_index("core")
    place = lax.axis_index("x")
    got = jnp.stack([part, send(part, "x", -1), send(part, "x", 2), send(part, "x", 1)])
    back = jnp.stack(
        [lax.dynamic_index_in_dim(got, lax.rem(k - place + 4, 4), 0, keepdims=False) for k in range(4)]
    )
    other = send(back, "core", 1)
    both = jnp.where(core == 0, jnp.stack([back, other]), jnp.stack([other, back]))
    return both.reshape(-1, part.shape[1])


def sum_over_cols(gram):
    core = lax.axis_index("core")
    halves = gram.reshape(2, -1, gram.shape[1])
    mine = lax.dynamic_index_in_dim(halves, core, 0, keepdims=False)
    theirs = lax.dynamic_index_in_dim(halves, 1 - core, 0, keepdims=False)
    mine = sum_direct(mine + send(theirs, "core", 1), "x")
    other = send(mine, "core", 1)
    return jnp.where(core == 0, jnp.stack([mine, other]), jnp.stack([other, mine])).reshape(gram.shape)


def product_kernel(transpose, spans, low, plain, coded, with_gram, count_ref, to_ref, from_ref, tiles, *rest):
    pieces, rest = rest[: len(spans)], rest[len(spans) :]
    outs, rest = rest[: 2 * len(plain) + len(coded) + with_gram], rest[2 * len(plain) + len(coded) + with_gram :]
    held, tiles_ref, total, slots, places, arrived, left = rest
    copies = [
        pltpu.make_async_copy(piece, held.at[pl.ds(start, length)], arrived.at[i])
        for i, (piece, (start, length)) in enumerate(zip(pieces, spans))
    ]
    copies.append(pltpu.make_async_copy(tiles, tiles_ref, arrived.at[len(pieces)]))
    for copy in copies:
        copy.start()
    total[...] = jnp.zeros_like(total)
    blocks_here = sum(plain) + sum(coded)

    def choose(i, found):
        place = to_ref[i] - low
        slots[found] = i
        places[found] = place
        return found + jnp.where((place >= 0) & (place < blocks_here), 1, 0)

    found = lax.fori_loop(0, count_ref[0], choose, 0)
    for j in range(GROUP):
        slots[found + j] = 0
        places[found + j] = blocks_here
    for copy in copies:
        copy.wait()
    dims = (((0,), (0,)), ((), ())) if transpose else (((1,), (0,)), ((), ()))

    def step(i, carry):
        products = []
        for j in range(GROUP):
            slot = slots[i * GROUP + j]
            products.append(
                lax.dot_general(tiles_ref[slot], held[from_ref[slot]], dims, preferred_element_type=f32)
            )
        for j in range(GROUP):
            total[places[i * GROUP + j]] += products[j]
        return carry

    lax.fori_loop(0, (found + GROUP - 1) // GROUP, step, 0)
    start = 0
    copies = []
    for k, blocks in enumerate(plain):
        copies.append(pltpu.make_async_copy(total.at[pl.ds(start, blocks)], outs[2 * k], left.at[k]))
        copies[-1].start()
        start += blocks

    def bound_of(start, blocks):
        def widen(i, bound):
            return jnp.maximum(bound, jnp.max(jnp.abs(total[start + i]), axis=0, keepdims=True))

        return lax.fori_loop(0, blocks, widen, jnp.zeros((1, total.shape[2]), f32))

    start = 0
    for k, blocks in enumerate(plain):
        bound_ref = outs[2 * k + 1]
        if transpose and k:
            bound_ref[...] = bound_of(start, blocks)
        else:
            bound_ref[...] = jnp.zeros_like(bound_ref)
        start += blocks
    tile = total.shape[1]
    for k, blocks in enumerate(coded):
        out_ref = outs[2 * len(plain) + k]
        power, scale = power_of(bound_of(start, blocks))

        def finish(i, carry, out_ref=out_ref, start=start, scale=scale):
            rows = pl.ds(pl.multiple_of(i * tile, tile), tile)
            out_ref[rows, :] = whole(total[start + i] * scale)
            return carry

        lax.fori_loop(0, blocks, finish, 0)
        out_ref[blocks * tile :, :] = jnp.broadcast_to(power, (TAIL, power.shape[1])).astype(jnp.int32).astype(jnp.int16)
        start += blocks
    if with_gram:
        gram_ref = outs[-1]
        gram_ref[...] = jnp.zeros_like(gram_ref)

        def add(i, carry):
            block = held[pl.ds(i * GROUP, GROUP)].reshape(GROUP * tile, -1)
            gram_ref[...] += lax.dot_general(block, block, (((0,), (0,)), ((), ())), preferred_element_type=f32)
            return carry

        lax.fori_loop(0, held.shape[0] // GROUP, add, 0)
    for copy in copies:
        copy.wait()


def product(tiles, pieces, to, source, count, low, plain, coded, transpose, with_gram=False):
    slots, tile, _ = tiles.shape
    width = pieces[0].shape[1]
    pieces = [piece.reshape(-1, tile, width) for piece in pieces]
    spans, start = [], 0
    for piece in pieces:
        spans.append((start, piece.shape[0]))
        start += piece.shape[0]
    outs = sum(plain) + sum(coded)
    smem = pl.BlockSpec(memory_space=pltpu.SMEM)
    vmem = pl.BlockSpec(memory_space=pltpu.VMEM)
    shapes = []
    for blocks in plain:
        shapes += [jax.ShapeDtypeStruct((blocks, tile, width), f32), jax.ShapeDtypeStruct((1, width), f32)]
    shapes += [jax.ShapeDtypeStruct((blocks * tile + TAIL, width), jnp.int16) for blocks in coded]
    shapes += [jax.ShapeDtypeStruct((width, width), f32)] * with_gram
    found = pl.pallas_call(
        functools.partial(product_kernel, transpose, tuple(spans), low, plain, coded, with_gram),
        out_shape=shapes,
        in_specs=[smem, smem, smem] + [pl.BlockSpec(memory_space=pl.ANY)] * (1 + len(pieces)),
        out_specs=[pl.BlockSpec(memory_space=pl.ANY), vmem] * len(plain) + [vmem] * (len(coded) + with_gram),
        scratch_shapes=[
            pltpu.VMEM((start, tile, width), bf16),
            pltpu.VMEM((slots, tile, tile), bf16),
            pltpu.VMEM((outs + 1, tile, width), f32),
            pltpu.SMEM((slots + GROUP,), jnp.int32),
            pltpu.SMEM((slots + GROUP,), jnp.int32),
            pltpu.SemaphoreType.DMA((len(pieces) + 1,)),
            pltpu.SemaphoreType.DMA((max(len(plain), 1),)),
        ],
        compiler_params=pltpu.CompilerParams(vmem_limit_bytes=48 * MIB),
        cost_estimate=pl.CostEstimate(
            flops=2 * slots * tile * tile * width,
            bytes_accessed=2 * (slots * tile * tile + (start + 2 * outs) * tile * width),
            transcendentals=0,
        ),
    )(count, to, source, tiles, *pieces)
    return [x.reshape(-1, width) for x in found]


def gram_of(panel):
    return lax.dot_general(panel, panel, (((0,), (0,)), ((), ())), precision=highest)


def apply_factor(panel, inverse):
    return lax.dot_general(panel, inverse, (((1,), (1,)), ((), ())), precision=highest)


def factor_kernel(gram_ref, out_ref, work):
    order = gram_ref.shape[0]
    shape = (BLOCK, 128)
    row_id = lax.broadcasted_iota(jnp.int32, shape, 0)
    unit = jnp.where(row_id == lax.broadcasted_iota(jnp.int32, shape, 1), 1.0, 0.0)
    work[:, :order] = gram_ref[...]
    square = (order, order)
    work[:, order:] = jnp.where(
        lax.broadcasted_iota(jnp.int32, square, 0) == lax.broadcasted_iota(jnp.int32, square, 1), 1.0, 0.0
    )
    for low in range(0, order, BLOCK):
        group = low // 128 * 128
        left = work[low : low + BLOCK, group : group + 128]
        right = unit
        pivots = jnp.ones(shape, f32)
        for start in range(0, BLOCK, PIVOTS):
            lane = low - group + start
            columns = [
                jnp.broadcast_to(left[:, lane + m : lane + m + 1], shape) for m in range(PIVOTS)
            ]
            for m in range(PIVOTS):
                at = start + m
                column = columns[m]
                pivot = jnp.broadcast_to(column[at : at + 1], shape)
                pivots = jnp.where(row_id == at, pivot, pivots)
                weight = jnp.where(row_id > at, column * (1.0 / pivot), 0.0)
                for q in range(m + 1, PIVOTS):
                    columns[q] = columns[q] - weight * column[start + q : start + q + 1]
                left = left - weight * left[at : at + 1]
                right = right - weight * right[at : at + 1]
        root = lax.rsqrt(pivots)
        root = root * (1.5 - 0.5 * pivots * root * root)
        right = right * root
        rows = jnp.dot(
            right[:, :BLOCK], work[low : low + BLOCK, :], precision=highest, preferred_element_type=f32
        )
        out_ref[low : low + BLOCK, :] = rows[:, order:]
        if low + BLOCK < order:
            update = lax.dot_general(
                rows[:, :order], rows, (((0,), (0,)), ((), ())), precision=highest, preferred_element_type=f32
            )
            work[low + BLOCK :, :] -= update[low + BLOCK :, :]


def inverse_factor(gram):
    order = gram.shape[0]
    return pl.pallas_call(
        factor_kernel,
        out_shape=jax.ShapeDtypeStruct(gram.shape, f32),
        scratch_shapes=[pltpu.VMEM((order, 2 * order), f32)],
        compiler_params=pltpu.CompilerParams(vmem_limit_bytes=16 * MIB),
        cost_estimate=pl.CostEstimate(flops=12 * GIGA, bytes_accessed=40 * MIB, transcendentals=0),
    )(gram)


def on_device(omega, tiles, coords):
    tile = tiles.shape[-1]
    factor = math.sqrt(omega.shape[0] * 256)
    local_tiles = tiles.reshape(tiles.shape[2], tile, tile)
    pairs = coords.reshape(coords.shape[2], 2)
    live = pairs[:, 0] >= 0
    count = jnp.sum(live.astype(jnp.int32)).reshape(1)
    my_y, my_z = lax.axis_index("y"), lax.axis_index("z")
    my_x, my_core = lax.axis_index("x"), lax.axis_index("core")

    local_row = jnp.clip(pairs[:, 0] - (my_y * 8 + my_z) * 16, 0, 15)
    keeper = local_row // 2
    row_slot = ((keeper + my_core) % 2 * 4 + (keeper // 2 - my_x + 4) % 4) * 2 + local_row % 2
    block_col = jnp.maximum(pairs[:, 1], 0)
    owner = block_col // 16
    far_y = (owner // 8 - my_y + 4) % 4
    far_z = (owner % 8 - my_z + 8) % 8
    panel_slot = jnp.where(block_col % 2 == 0, far_y * 8 + owner % 8, 32 + far_z * 4 + far_y)
    order_y = jnp.where(far_y == 2, 3, jnp.where(far_y == 3, 2, far_y))
    column_slot = (order_y * 8 + owner % 8) * 2 + block_col % 2
    row_to = jnp.where(live, row_slot, 16)
    column_to = jnp.where(live, column_slot, 64)

    def forward(panel, with_gram=False):
        pieces = gather_rows(panel.astype(bf16))
        return product(local_tiles, pieces, row_to, panel_slot, count, 0, (8, 8), (), False, with_gram)

    one = sum_cols(exchange_cols(forward(omega)))
    magnitude = jnp.max(jnp.where(live, jnp.max(jnp.abs(local_tiles), axis=(1, 2)).astype(f32), 0.0))
    scale = jnp.exp2(-power_of(largest_everywhere(magnitude))[0])
    pieces = gather_cols((one * scale).astype(bf16))
    far = product(local_tiles, pieces, column_to, row_slot, count, 48, (), (8, 8), True)
    *far, pieces[0], held_back = together(*far, pieces[0], one)
    first, second = send(far[0], "y", 1), send(far[1], "y", -1)
    shares = product(local_tiles, pieces, column_to, row_slot, count, 0, (16, 16, 16), (), True)
    gram = gram_over_core(gram_of(held_back))
    first, second, gram, *shares = together(first, second, gram, *shares)
    total, one_inverse = sum_rows(first, second, shares, gram)
    two = apply_factor(total, one_inverse)
    *shares, gram = forward(two, True)
    parts = exchange_cols(shares)
    gram, *parts = together(sum_over_cols(gram), *parts)
    two_inverse = inverse_factor(gram)
    three = apply_factor(sum_cols(parts), two_inverse)
    three_inverse = inverse_factor(sum_everywhere(gram_of(three)))
    return (
        apply_factor(three, three_inverse) * factor,
        apply_factor(one, one_inverse) * factor,
        apply_factor(two, two_inverse) * factor,
    )


def solution(mesh):
    mesh = Mesh(mesh.devices.reshape([SIZE[name] for name in AXES]), AXES)
    rows, cols = ("y", "z"), ("x", "core")
    return jax.shard_map(
        on_device,
        mesh=mesh,
        in_specs=(P(AXES, None), P(rows, cols, None, None, None), P(rows, cols, None, None)),
        out_specs=(P(AXES, None),) * 3,
        check_vma=False,
    )
```
